128 devices in a mesh: segment: 4 (over y), dp: 32 (over z, x, core).
Axes of the slice: x: 4, y: 4, z: 4, core: 2. Of those that a mesh axis runs over, the one named last changes fastest.
Arguments:
- inputs: bfloat16 [14336, 8192], P('dp'), may hold values from -6 to 6
- cotangent: bfloat16 [14336, 8192], P('dp'), may hold values from -11 to 11
- adapter_down: bfloat16 [4, 128, 8192], P('segment'), may hold values from -0.0625 to 0.0625
- adapter_up: bfloat16 [4, 8192, 128], P('segment'), may hold values from -0.5 to 0.5
- domain_ids: int32 [256], replicated, may hold values from 0 to 8, as said below
- prior_weights: float32 [8], replicated, may hold values from 0.2 to 1
Outputs:
- domain_weights: float32 [8], replicated
- reweighted: float32 [4, 128, 8192], P('segment', None, 'dp')
The draws below stay inside these ranges and needn't reach their ends.
Inputs may be any that keep to these rules, and one draw needn't show every extreme that they name: `domain_ids`: each of the 9 domains names 28 or 29 micro-batches; domain 8 is the generalization domain.
All inputs are finite; a program needn't handle non-finite values.
Results may differ from the reference program's by a relative error of at most 0.02.
Values may be sent and summed in bfloat16 or wider, within the bound.
A program may use at most 128 MiB of HBM per device.

```python
import math
import jax
import jax.numpy as jnp
from jax import lax

D = 8192
RANK = 128
DOMAINS = 9
MICRO_DEV = 8
TOK_MICRO = 56
TRAIN = 8
SEGMENTS = 4
MICROS = 256
TOKENS = 14336
N_DP = 32


def draw_domain_ids(key, part):
    order = jax.random.permutation(jax.random.fold_in(key, 11), MICROS)
    return (order % DOMAINS).astype(jnp.int32)


def draw_cotangent(key, part):
    noise_key = jax.random.fold_in(key, 23)
    row_place = jnp.arange(TOKENS, dtype=jnp.float32) / TOKENS
    base = jnp.clip(jax.random.normal(noise_key, (TOKENS, D), jnp.float32), -6.0, 6.0)
    return (base * (3.0 ** row_place)[:, None] / 1.7).astype(jnp.bfloat16)


def shard_levels(key, dims, split, low, largest):
    factor_of, own = 1.0, jax.random.fold_in(key, 6)
    for position, parts in split:
        draws = jnp.exp(jax.random.uniform(jax.random.fold_in(own, position), (parts,), jnp.float32, low / len(split), largest / len(split)))
        factor_of = factor_of * jnp.repeat(draws, dims[position] // parts).reshape([-1 if axis == position else 1 for axis in range(len(dims))])
    return factor_of


def noise(key, shape, width, most, shards=(), held_as=jnp.bfloat16):
    result = width * jax.random.normal(key, shape, jnp.float32)
    if shards:
        result = result * shard_levels(key, shape, shards, -0.22, 0.18)
    return jnp.clip(result, -most, most).astype(held_as)


def setup_inputs(seed: int = 0) -> dict:
    splits = jax.random.split(jax.random.key(seed), 7)
    return {
        "inputs": noise(splits[0], (TOKENS, D), 1.0, 6.0, ((0, 32),)),
        "cotangent": draw_cotangent(jax.random.fold_in(splits[6], 71), 0),
        "adapter_down": noise(splits[2], (SEGMENTS, RANK, D), D ** -0.5, 0.0625, ((0, 4),)),
        "adapter_up": noise(splits[3], (SEGMENTS, D, RANK), RANK ** -0.5, 0.5, ((0, 4),)),
        "domain_ids": draw_domain_ids(jax.random.fold_in(splits[6], 71), 0),
        "prior_weights": jnp.clip(jnp.exp(jax.random.uniform(splits[5], (TRAIN,), jnp.float32, math.log(0.2), math.log(1.0))), 0.2, 1.0),
    }


smoothing = 0.5

def silu_slope(preact):
    sigmoid_value = jax.nn.sigmoid(preact)
    return sigmoid_value * (1.0 + preact * (1.0 - sigmoid_value))

def reference(inputs, cotangent, adapter_down, adapter_up, domain_ids, prior_weights):
    segment_inputs = []
    segment_pre = []
    current = inputs
    for section in range(SEGMENTS):
        hidden_pre = jnp.dot(current, adapter_down[section].T, preferred_element_type=jnp.float32)
        hidden_act = jax.nn.silu(hidden_pre).astype(jnp.bfloat16)
        segment_inputs.append(current)
        segment_pre.append(hidden_pre)
        lifted = jnp.dot(hidden_act, adapter_up[section].T, preferred_element_type=jnp.float32)
        current = (current.astype(jnp.float32) + lifted).astype(jnp.bfloat16)
    delta_block = cotangent
    inner_list = [None] * SEGMENTS
    for section in reversed(range(SEGMENTS)):
        pulled_back = jnp.dot(delta_block, adapter_up[section], preferred_element_type=jnp.float32)
        inner_grad = (pulled_back * silu_slope(segment_pre[section])).astype(jnp.bfloat16)
        inner_list[section] = inner_grad
        pushed = jnp.dot(inner_grad, adapter_down[section], preferred_element_type=jnp.float32)
        delta_block = (delta_block.astype(jnp.float32) + pushed).astype(jnp.bfloat16)
    domain_range = jnp.arange(DOMAINS, dtype=jnp.int32)
    onehot = (domain_ids[:, None] == domain_range[None, :]).astype(jnp.float32)
    counts = lax.optimization_barrier(jnp.sum(onehot, axis=0))
    inverse_size = 1.0 / (counts * TOK_MICRO)
    micro_mix = (onehot * inverse_size[None, :]).reshape(N_DP, MICRO_DEV, DOMAINS)
    stacked_inputs = jnp.stack(segment_inputs).reshape(SEGMENTS, N_DP, MICRO_DEV, TOK_MICRO, D)
    stacked_inner = jnp.stack(inner_list).reshape(SEGMENTS, N_DP, MICRO_DEV, TOK_MICRO, RANK)

    def add_owner(total_grad, owner_slot):
        owner_parts = []
        for section in range(SEGMENTS):
            per_micro = jnp.einsum('mtr,mtd->mrd', stacked_inner[section, owner_slot].astype(jnp.float32), stacked_inputs[section, owner_slot].astype(jnp.float32), precision=lax.Precision.HIGHEST)
            owner_part = jnp.einsum('mi,mrd->ird', micro_mix[owner_slot], per_micro, precision=lax.Precision.HIGHEST).astype(jnp.bfloat16)
            owner_part = lax.optimization_barrier(owner_part)
            owner_parts.append(owner_part.astype(jnp.float32))
        return (total_grad + jnp.stack(owner_parts), None)
    zero_grad = jnp.zeros((SEGMENTS, DOMAINS, RANK, D), jnp.float32)
    total_grad, _ = lax.scan(add_owner, zero_grad, jnp.arange(N_DP, dtype=jnp.int32))
    train_grads = total_grad[:, :DOMAINS - 1]
    gen_grad = total_grad[:, DOMAINS - 1]
    scores = lax.optimization_barrier(jnp.sum(train_grads * gen_grad[:, None], axis=(0, 2, 3)))
    mean_gen = jnp.mean(gen_grad * gen_grad)
    total_entries = SEGMENTS * RANK * D
    scaled_scores = scores / (jnp.sqrt(jnp.float32(total_entries)) * (mean_gen + 1e-06))
    raised = prior_weights * jnp.exp(4.0 * jnp.tanh(scaled_scores / 4.0))
    weights_new = smoothing / (DOMAINS - 1) + (1.0 - smoothing) * raised / jnp.sum(raised)
    reweighted = jnp.einsum('i,sird->srd', weights_new, train_grads, precision=lax.Precision.HIGHEST)
    return (weights_new, reweighted)
```

```python
import functools
import math

import jax
import jax.numpy as jnp
from jax import lax
from jax.experimental import pallas as pl
from jax.experimental.pallas import tpu as pltpu
from jax.sharding import PartitionSpec as P

DOMAINS = 9
TOK_MICRO = 56
SMOOTHING = 0.5
MESH = pl.DeviceIdType.MESH
F32 = jnp.float32
BF16 = jnp.bfloat16
NT = (((1,), (1,)), ((), ()))
NN = (((1,), (0,)), ((), ()))
TN = (((0,), (0,)), ((), ()))


def dot(a, b, dims):
    return lax.dot_general(a, b, dims, preferred_element_type=F32)


def remote(src, dst, send, recv, seg, dp):
    return pltpu.make_async_remote_copy(
        src_ref=src, dst_ref=dst, send_sem=send, recv_sem=recv, device_id=(seg, dp), device_id_type=MESH
    )


def each(lo, hi, body):
    def step(i, carry):
        body(i)
        return carry

    lax.fori_loop(lo, hi, step, 0)


def kernel(
    x_hbm, cot_hbm, down_hbm, up_hbm, ids, prior,
    wout, rout,
    xv, cv, dv, uv, acc, e_up, e_dn, e_cat, e_part, e_rs, e_seg, e_all, a_all, b_all, act_cat, inner_cat,
    up_cat, xs, hot, col8, lhs_t, cross,
    g_send, g_ra, g_rb, g_sa, g_sb, g_ra2, g_rb2, g_all, sc0, sc1, sc1s, sc2,
    f_send, f_ra, f_rb, f_sa, f_sb, f_ra2, f_rb2,
    s_x, s_c, s_d, s_u, s_loc,
    eu_s, eu_r, ed_s, ed_r, er_s, er_r, ey_s, ey_r, ea_s, ea_r, ep_s, ep_r,
    a_s, a_r, b_s, b_r, ue_s, ue_r, xp_s, xp_r, ac_s, ac_r, in_s, in_r,
    g_s, g_r, h_s, h_r, p_s, p_r, q_s, q_r, f_s, f_r,
):
    n_seg = 4
    n_chip = e_part.shape[0]
    n_x = n_chip // n_seg
    tokens, width = x_hbm.shape
    rank = down_hbm.shape[0]
    block = width // (2 * n_chip)
    cols = n_x * block
    chunks = s_x.shape[0]
    kc = width // chunks
    half = rank // 2
    low, high = pl.ds(0, half), pl.ds(half, half)
    piece = width // (n_seg * n_chip)
    per = block // piece

    r = lax.axis_index("segment")
    dp = lax.axis_index("dp")
    c = dp % 2
    k = dp // 2
    z = k // n_x
    xx = k % n_x
    oc = 1 - c
    partner = k * 2 + oc
    up_core = (k // per) % 2

    def chip(n):
        return n * 2 + c

    bar = pltpu.get_barrier_semaphore()

    def greet(seg, d):
        pl.semaphore_signal(bar, inc=1, device_id=(seg, d), device_id_type=MESH)

    def greet_plane(i):
        greet(r, chip((k + i) % n_chip))

    each(1, n_chip, greet_plane)

    def greet_seg(i):
        greet((r + i) % n_seg, dp)
        greet((r + i) % n_seg, partner)

    each(1, n_seg, greet_seg)
    greet(r, partner)

    not_diag = z != r
    for i in range(n_seg):
        j = (z + i) % n_seg
        if i == 0:
            @pl.when(not_diag)
            def _():
                greet(z, chip(r * n_x + xx))
                greet(z, chip(r * n_x + xx))
        else:
            greet(j, chip(r * n_x + xx))
        j = (r + i) % n_seg
        if i == 0:
            @pl.when(not_diag)
            def _():
                greet(z, chip(r * n_x + xx))
                greet(z, chip(r * n_x + xx))
        else:
            greet(z, chip(j * n_x + xx))
    for i in range(1, n_x):
        j = (xx + i) % n_x
        greet(z, chip(r * n_x + j))
        greet(z, chip(r * n_x + j))

    def piece_of(seg):
        return pl.ds(pl.multiple_of((seg * n_chip + k) * piece, 128), piece)

    def own_dn():
        return pltpu.make_async_copy(down_hbm.at[:, piece_of(r)], e_dn.at[r], s_loc.at[0])

    def own_up():
        return pltpu.make_async_copy(up_hbm.at[piece_of(r), :], e_up.at[r], s_loc.at[1])

    own_dn().start()
    own_up().start()
    pltpu.make_async_copy(down_hbm, dv, s_d).start()

    def x_copy(i):
        sl = pl.ds(i * kc, kc)
        return pltpu.make_async_copy(x_hbm.at[:, sl], xv.at[:, sl], s_x.at[i])

    def c_copy(i):
        sl = pl.ds(i * kc, kc)
        return pltpu.make_async_copy(cot_hbm.at[:, sl], cv.at[:, sl], s_c.at[i])

    each(0, chunks, lambda i: x_copy(i).start())
    pltpu.make_async_copy(up_hbm, uv, s_u).start()
    each(0, chunks, lambda i: c_copy(i).start())

    def own_cols(i, core):
        return pl.ds(((r * n_x + i) * 2 + core) * block, block)

    def xe_copy(i):
        return pltpu.make_async_copy(
            x_hbm.at[:, own_cols(i, c)], xs.at[c, :, pl.ds(i * block, block)], s_loc.at[2 + i]
        )

    each(0, n_x, lambda i: xe_copy(i).start())

    lane = lax.broadcasted_iota(jnp.int32, (1, 128), 1)

    def count(i, total):
        return total + jnp.where(lane == ids[i], 1.0, 0.0)

    counts = lax.fori_loop(0, ids.shape[0], count, jnp.zeros((1, 128), F32))
    scale = 1.0 / (counts * TOK_MICRO)
    micros = 2 * tokens // TOK_MICRO

    def fill(m):
        name = ids[k * micros + m]
        row = jnp.where(lane == name, scale, 0.0)
        hot[pl.ds(pl.multiple_of(m * TOK_MICRO, 8), TOK_MICRO), :] = jnp.broadcast_to(row, (TOK_MICRO, 128))

    each(0, micros, fill)
    lanes_full = lax.broadcasted_iota(jnp.int32, (2 * tokens, 128), 1)
    only8 = jnp.where(lanes_full == DOMAINS - 1, hot[...], 0.0)
    col8[...] = jnp.broadcast_to(jnp.sum(only8, axis=1, keepdims=True), (2 * tokens, 128))

    pl.semaphore_wait(bar, (n_chip - 1) + 2 * (n_seg - 1) + 1 + 2 * (n_seg + n_x) - jnp.where(not_diag, 0, 4))

    def e_up_from(j):
        return (j < n_seg - 1) & ((c == 0) & (j == 0) | (c == 1) & (j >= 1) | (c == up_core))

    def e_dn_from(j):
        return j >= 1 + c

    def e_up_copy(slot, peer):
        return remote(up_hbm.at[piece_of(peer), :], e_up.at[slot], eu_s.at[peer], eu_r.at[slot], peer, dp)

    def e_dn_copy(slot, peer):
        return remote(down_hbm.at[:, piece_of(peer)], e_dn.at[slot], ed_s.at[peer], ed_r.at[slot], peer, dp)

    for i in range(1, n_seg):
        peer = (r + i) % n_seg

        @pl.when(e_up_from(r))
        def _():
            e_up_copy(r, peer).start()

        @pl.when(e_dn_from(r))
        def _():
            e_dn_copy(r, peer).start()

    def xp_copy(i, slot_core, col_core):
        return remote(
            x_hbm.at[:, own_cols(i, col_core)],
            xs.at[slot_core, :, pl.ds(i * block, block)],
            xp_s.at[i],
            xp_r.at[i],
            r,
            partner,
        )

    each(0, n_x, lambda i: xp_copy(i, c, oc).start())

    pltpu.make_async_copy(down_hbm, dv, s_d).wait()
    acc[...] = jnp.zeros_like(acc)

    def a_step(i):
        x_copy(i).wait()
        sl = pl.ds(pl.multiple_of(i * kc, 128), kc)
        acc[...] += dot(xv[:, sl], dv[:, sl], NT)

    each(0, chunks, a_step)
    a_all[r] = acc[...].astype(BF16)

    def seg_copy(buf, send, recv, slot, peer):
        return remote(buf.at[slot], buf.at[slot], send.at[peer], recv.at[slot], peer, dp)

    for i in range(1, n_seg):
        seg_copy(a_all, a_s, a_r, r, (r + i) % n_seg).start()

    for j in range(n_seg):
        @pl.when((j != r) & e_up_from(j))
        def _():
            e_up_copy(j, (r + 1) % n_seg).wait_recv()

        @pl.when((j != r) & e_dn_from(j))
        def _():
            e_dn_copy(j, (r + 1) % n_seg).wait_recv()

    own_dn().wait()
    own_up().wait()
    e_rows = e_part.shape[1]
    e_mats = []
    for m, (da, ua) in enumerate(((2, 1), (3, 1), (3, 2))):
        e_mats.append(dot(e_dn[(1 - c) * (m + 1) + c * da], e_up[c * ua], NN))
    e_part[...] = jnp.concatenate(e_mats, axis=0).reshape(n_chip, e_rows, rank)

    def er_copy(slot, n):
        return remote(e_part.at[n], e_rs.at[slot], er_s.at[n], er_r.at[slot], r, chip(n))

    each(1, n_chip, lambda i: er_copy(k, (k + i) % n_chip).start())

    def up_slot(n):
        return up_cat.at[n // (2 * per), pl.ds(pl.multiple_of((n % per) * piece, 128), piece)]

    def ue_copy(slot, n):
        return remote(e_cat, up_slot(slot), ue_s.at[n], ue_r.at[slot], r, chip(n))

    @pl.when(c == up_core)
    def _():
        for j in range(n_seg - 1):
            e_cat[:, j * rank:(j + 1) * rank] = e_up[j]
        each(1, n_chip, lambda i: ue_copy(k, (k + i) % n_chip).start())
        up_cat[k // (2 * per), pl.ds(pl.multiple_of((k % per) * piece, 128), piece)] = e_cat[...]

    pltpu.make_async_copy(up_hbm, uv, s_u).wait()
    acc[...] = jnp.zeros_like(acc)

    def b_step(i):
        c_copy(i).wait()
        sl = pl.ds(pl.multiple_of(i * kc, 128), kc)
        acc[...] += dot(cv[:, sl], uv[sl, :], NN)

    each(0, chunks, b_step)
    b_all[r] = acc[...].astype(BF16)
    for i in range(1, n_seg):
        seg_copy(b_all, b_s, b_r, r, (r + i) % n_seg).start()

    def er_sum(i, total):
        n = (k + i) % n_chip
        er_copy(n, n).wait_recv()
        return total + e_rs[n]

    e_seg[r] = lax.fori_loop(1, n_chip, er_sum, e_part[k])
    for i in range(1, n_seg):
        seg_copy(e_seg, ey_s, ey_r, r, (r + i) % n_seg).start()
    for i in range(1, n_seg):
        j = (r + i) % n_seg
        seg_copy(e_seg, ey_s, ey_r, j, j).wait_recv()
    e_all[c, k] = e_seg[0] + e_seg[1] + e_seg[2] + e_seg[3]

    def ea_copy(slot, n):
        return remote(e_all.at[c, slot], e_all.at[c, slot], ea_s.at[n], ea_r.at[slot], r, chip(n))

    each(1, n_chip, lambda i: ea_copy(k, (k + i) % n_chip).start())

    def ea_wait(i):
        n = (k + i) % n_chip
        ea_copy(n, n).wait_recv()

    each(1, n_chip, ea_wait)

    def ep_copy(core):
        return remote(e_all.at[core], e_all.at[core], ep_s, ep_r, r, partner)

    ep_copy(c).start()
    ep_copy(oc).wait_recv()

    for i in range(1, n_seg):
        j = (r + i) % n_seg
        seg_copy(a_all, a_s, a_r, j, j).wait_recv()

    e0 = e_all[0].reshape(3 * rank, rank).astype(BF16)
    e1 = e_all[1].reshape(3 * rank, rank).astype(BF16)
    e10, e20, e30 = e0[:rank], e0[rank:2 * rank], e0[2 * rank:]
    e21, e31, e32 = e1[:rank], e1[rank:2 * rank], e1[2 * rank:]

    def act_copy(j, core):
        ref = act_cat.at[core, :, pl.ds(j * rank, rank)]
        return remote(ref, ref, ac_s.at[j], ac_r.at[j], r, partner)

    def in_copy(j, core):
        ref = inner_cat.at[core, :, pl.ds(j * rank, rank)]
        return remote(ref, ref, in_s.at[j], in_r.at[j], r, partner)

    slopes = []
    acts = []
    lower = {(1, 0): e10, (2, 0): e20, (2, 1): e21, (3, 0): e30, (3, 1): e31, (3, 2): e32}
    for s in range(n_seg):
        pre = a_all[s].astype(F32)
        for j in range(s):
            pre = pre + dot(acts[j], lower[(s, j)], NT)
        sig = 1.0 / (1.0 + jnp.exp(-pre))
        slopes.append(sig * (1.0 + pre * (1.0 - sig)))
        if s < n_seg - 1:
            act = (pre * sig).astype(BF16)
            acts.append(act)
            act_cat[c, :, s * rank:(s + 1) * rank] = act
            act_copy(s, c).start()

    for i in range(1, n_seg):
        j = (r + i) % n_seg
        seg_copy(b_all, b_s, b_r, j, j).wait_recv()

    inners = [None] * n_seg
    for s in reversed(range(n_seg)):
        pulled = b_all[s].astype(F32)
        for j in range(s + 1, n_seg):
            pulled = pulled + dot(inners[j], lower[(j, s)], NN)
        inner = (pulled * slopes[s]).astype(BF16)
        inners[s] = inner
        inner_cat[c, :, s * rank:(s + 1) * rank] = inner
        in_copy(s, c).start()

    each(0, n_x, lambda i: xe_copy(i).wait())
    each(0, n_x, lambda i: xp_copy(i, oc, c).wait_recv())

    def ue_wait(i):
        n = (k + i) % n_chip

        @pl.when((n // per) % 2 == c)
        def _():
            ue_copy(n, n).wait_recv()

    each(1, n_chip, ue_wait)
    for s in range(n_seg - 1):
        act_copy(s, oc).wait_recv()
    for s in range(n_seg):
        in_copy(s, oc).wait_recv()
    stack = n_seg * rank
    lower_mask = (
        lax.broadcasted_iota(jnp.int32, (stack, stack - rank), 0) // rank
        > lax.broadcasted_iota(jnp.int32, (stack, stack - rank), 1) // rank
    )

    def set_weighted():
        for h in range(2):
            weight = col8[pl.ds(h * tokens, tokens), :]
            for s in range(n_seg):
                weighted = inner_cat[h, :, s * rank:(s + 1) * rank].astype(F32) * weight
                lhs_t[h, s * rank:(s + 1) * rank, :] = weighted.T.astype(BF16)
        both = dot(lhs_t[0], act_cat[0], NN) + dot(lhs_t[1], act_cat[1], NN)
        cross[...] = jnp.where(lower_mask, both, 0.0).astype(BF16)

    def weighted_grad(i):
        sl = pl.ds(pl.multiple_of(i * block, 128), block)
        total = dot(lhs_t[0], xs[0, :, sl], NN) + dot(lhs_t[1], xs[1, :, sl], NN)
        return total + dot(cross[...], up_cat[i], NT)

    def x_peer(i):
        return (xx + i) % n_x

    def z_peer(i):
        return (z + i) % n_seg

    def first_a(send, recv, ss, rs, slot, i):
        return remote(send.at[i, :, low], recv.at[slot], ss.at[0, i], rs.at[0, slot], r, chip(z * n_x + i))

    def first_b(send, recv, ss, rs, slot, j):
        return remote(send.at[:, j, high], recv.at[slot], ss.at[1, j], rs.at[1, slot], r, chip(j * n_x + xx))

    def spread(send, recv_a, recv_b, ss, rs):
        set_weighted()

        def column_block(t):
            i = (xx + 1 + t) % n_x
            send[i] = weighted_grad(i).reshape(n_seg, rank, block).astype(BF16)

            @pl.when(i != xx)
            def _():
                first_a(send, recv_a, ss, rs, xx, i).start()

        each(0, n_x, column_block)
        for t in range(1, n_seg):
            first_b(send, recv_b, ss, rs, z, z_peer(t)).start()

    def sum_a(send, recv_a, ss, rs):
        total = send[xx, :, :half].astype(F32)
        for t in range(1, n_x):
            i = x_peer(t)
            first_a(send, recv_a, ss, rs, i, i).wait_recv()
            total = total + recv_a[i].astype(F32)
        return total.astype(BF16)

    def sum_b(send, recv_b, ss, rs):
        total = send[:, z, half:].astype(F32)
        for t in range(1, n_seg):
            j = z_peer(t)
            first_b(send, recv_b, ss, rs, j, j).wait_recv()
            total = total + recv_b[j].astype(F32)
        return total.astype(BF16)

    spread(g_send, g_ra, g_rb, g_s, g_r)
    g_sa[...] = sum_a(g_send, g_ra, g_s, g_r)

    def second_a(slot, j):
        return remote(g_sa.at[j], g_ra2.at[slot], g_s.at[2, j], g_r.at[2, slot], r, chip(j * n_x + xx))

    def second_b(slot, i):
        return remote(g_sb.at[i], g_rb2.at[slot], g_s.at[3, i], g_r.at[3, slot], r, chip(z * n_x + i))

    for t in range(1, n_seg):
        second_a(z, z_peer(t)).start()
    g_sb[...] = sum_b(g_send, g_rb, g_s, g_r)
    for t in range(1, n_x):
        second_b(xx, x_peer(t)).start()
    total = g_sa[z].astype(F32)
    for t in range(1, n_seg):
        j = z_peer(t)
        second_a(j, j).wait_recv()
        total = total + g_ra2[j].astype(F32)
    g_all[xx, z, :half] = total.astype(BF16)

    def gather(stage, slot, i, j):
        if stage == 0:
            ref, to = g_all.at[slot, z, low], z * n_x + i
        elif stage == 1:
            ref, to = g_all.at[xx, slot, high], j * n_x + xx
        elif stage == 2:
            ref, to = g_all.at[:, slot, low], j * n_x + xx
        else:
            ref, to = g_all.at[slot, :, high], z * n_x + i
        return remote(ref, ref, h_s.at[stage, i if stage in (0, 3) else j], h_r.at[stage, slot], r, chip(to))

    for t in range(1, n_x):
        gather(0, xx, x_peer(t), z).start()
    total = g_sb[xx].astype(F32)
    for t in range(1, n_x):
        i = x_peer(t)
        second_b(i, i).wait_recv()
        total = total + g_rb2[i].astype(F32)
    g_all[xx, z, half:] = total.astype(BF16)
    for t in range(1, n_seg):
        gather(1, z, xx, z_peer(t)).start()

    for t in range(1, n_x):
        gather(0, x_peer(t), xx, z).wait_recv()
    for t in range(1, n_seg):
        gather(2, z, xx, z_peer(t)).start()
    for t in range(1, n_seg):
        gather(1, z_peer(t), xx, z).wait_recv()
    for t in range(1, n_x):
        gather(3, xx, x_peer(t), z).start()
    for t in range(1, n_seg):
        gather(2, z_peer(t), xx, z).wait_recv()

    y0 = jnp.zeros((tokens, stack), F32)
    y1 = jnp.zeros((tokens, stack), F32)
    gu = jnp.zeros((stack, stack - rank), F32)
    for t in range(n_x):
        i = x_peer(t)
        if t:
            gather(3, i, xx, z).wait_recv()
        grad = g_all[i].reshape(stack, block)
        sl = pl.ds(pl.multiple_of(i * block, 128), block)
        y0 = y0 + dot(xs[0, :, sl], grad, NT)
        y1 = y1 + dot(xs[1, :, sl], grad, NT)
        gu = gu + dot(grad, up_cat[i], NN)
    gu = jnp.where(lower_mask, gu, 0.0).astype(BF16)
    mine = jnp.zeros((1, 128), F32)
    for h, y in ((0, y0), (1, y1)):
        y = (y + dot(act_cat[h], gu, NT)) * inner_cat[h].astype(F32)
        row = jnp.sum(y, axis=1, keepdims=True)
        mine = mine + jnp.sum(hot[h * tokens:(h + 1) * tokens, :] * row, axis=0, keepdims=True)
    sc0[...] = jnp.broadcast_to(mine, (8, 128))

    def p_copy(slot, n):
        return remote(sc0, sc1.at[slot], p_s.at[n], p_r.at[slot], r, chip(n))

    each(1, n_chip, lambda i: p_copy(k, (k + i) % n_chip).start())

    def p_sum(i, total):
        n = (k + i) % n_chip
        p_copy(n, n).wait_recv()
        return total + sc1[n]

    plane = lax.fori_loop(1, n_chip, p_sum, sc0[...])
    sc1s[...] = plane

    def q_copy(slot, n):
        return remote(sc1s, sc2.at[slot], q_s.at[n], q_r.at[slot], n // 2, k * 2 + n % 2)

    here = r * 2 + c
    each(1, 2 * n_seg, lambda i: q_copy(here, (here + i) % (2 * n_seg)).start())
    sc2[here] = plane

    def q_wait(i):
        n = (here + i) % (2 * n_seg)
        q_copy(n, n).wait_recv()

    each(1, 2 * n_seg, q_wait)
    scores = sc2[0]
    for n in range(1, 2 * n_seg):
        scores = scores + sc2[n]

    lane8 = lax.broadcasted_iota(jnp.int32, (8, 128), 1)
    entries = n_seg * rank * width
    mean_gen = jnp.sum(jnp.where(lane8 == DOMAINS - 1, scores, 0.0), axis=1, keepdims=True) / entries
    zed = scores / (math.sqrt(entries) * (mean_gen + 1e-06))
    prior_row = jnp.zeros((8, 128), F32)
    for i in range(DOMAINS - 1):
        prior_row = jnp.where(lane8 == i, prior[i], prior_row)
    train = lane8 < DOMAINS - 1
    raised = jnp.where(train, prior_row * jnp.exp(4.0 * jnp.tanh(zed / 4.0)), 0.0)
    weights = SMOOTHING / (DOMAINS - 1) + (1.0 - SMOOTHING) * raised / jnp.sum(raised, axis=1, keepdims=True)
    weights = jnp.where(train, weights, 0.0)
    token_weight = jnp.sum(hot[...] * weights[0:1], axis=1, keepdims=True)
    col8[...] = jnp.broadcast_to(token_weight, (2 * tokens, 128))

    spread(f_send, f_ra, f_rb, f_s, f_r)
    for i in range(DOMAINS - 1):
        wout[i] = jnp.sum(jnp.where(lane == i, weights[0:1], 0.0))

    def last_a(slot, s):
        return remote(f_sa.at[s], f_ra2.at[slot], f_s.at[2, s], f_r.at[2, slot], s, chip(r * n_x + xx))

    def last_b(slot, i):
        return remote(f_sb.at[i], f_rb2.at[slot], f_s.at[3, i], f_r.at[3, slot], z, chip(r * n_x + i))

    f_sa[...] = sum_a(f_send, f_ra, f_s, f_r)
    for t in range(1, n_seg):
        last_a(z, z_peer(t)).start()

    @pl.when(not_diag)
    def _():
        last_a(z, z).start()

    @pl.when(z == r)
    def _():
        f_ra2[z] = f_sa[z]

    f_sb[...] = sum_b(f_send, f_rb, f_s, f_r)
    for t in range(1, n_x):
        last_b(xx, x_peer(t)).start()

    @pl.when(not_diag)
    def _():
        last_b(xx, xx).start()

    @pl.when(z == r)
    def _():
        f_rb2[xx] = f_sb[xx]

    for t in range(1, n_seg):
        j = (r + t) % n_seg
        last_a(j, j).wait_recv()

    @pl.when(not_diag)
    def _():
        last_a(r, r).wait_recv()

    rout[:half] = sum(f_ra2[j].astype(F32) for j in range(n_seg))
    for t in range(1, n_x):
        i = x_peer(t)
        last_b(i, i).wait_recv()

    @pl.when(not_diag)
    def _():
        last_b(xx, xx).wait_recv()

    rout[half:] = sum(f_rb2[i].astype(F32) for i in range(n_x))

    for i in range(1, n_seg):
        peer = (r + i) % n_seg

        @pl.when(e_up_from(r))
        def _():
            e_up_copy(r, peer).wait_send()

        @pl.when(e_dn_from(r))
        def _():
            e_dn_copy(r, peer).wait_send()

        seg_copy(a_all, a_s, a_r, r, peer).wait_send()
        seg_copy(b_all, b_s, b_r, r, peer).wait_send()

        seg_copy(e_seg, ey_s, ey_r, r, peer).wait_send()

    each(0, n_x, lambda i: xp_copy(i, c, oc).wait_send())
    ep_copy(c).wait_send()
    each(0, n_seg - 1, lambda j: act_copy(j, c).wait_send())
    each(0, n_seg, lambda j: in_copy(j, c).wait_send())

    def plane_sent(i):
        n = (k + i) % n_chip
        er_copy(k, n).wait_send()
        ea_copy(k, n).wait_send()
        p_copy(k, n).wait_send()

    each(1, n_chip, plane_sent)

    @pl.when(c == up_core)
    def _():
        each(1, n_chip, lambda i: ue_copy(k, (k + i) % n_chip).wait_send())

    each(1, 2 * n_seg, lambda i: q_copy(here, (here + i) % (2 * n_seg)).wait_send())

    for t in range(1, n_x):
        i = x_peer(t)
        first_a(g_send, g_ra, g_s, g_r, xx, i).wait_send()
        first_a(f_send, f_ra, f_s, f_r, xx, i).wait_send()
        second_b(xx, i).wait_send()
        gather(0, xx, i, z).wait_send()
        gather(3, xx, i, z).wait_send()
        last_b(xx, i).wait_send()
    for t in range(1, n_seg):
        j = z_peer(t)
        first_b(g_send, g_rb, g_s, g_r, z, j).wait_send()
        first_b(f_send, f_rb, f_s, f_r, z, j).wait_send()
        second_a(z, j).wait_send()
        gather(1, z, xx, j).wait_send()
        gather(2, z, xx, j).wait_send()
        last_a(z, j).wait_send()

    @pl.when(not_diag)
    def _():
        last_a(z, z).wait_send()
        last_b(xx, xx).wait_send()


def local(n_dp, inputs, cotangent, adapter_down, adapter_up, domain_ids, prior_weights):
    n_seg = 4
    n_chip = n_dp // 2
    n_x = n_chip // n_seg
    tokens, width = inputs.shape
    rank = adapter_down.shape[1]
    block = width // n_dp
    cols = n_x * block
    chunks = 8
    half = rank // 2
    e_rows = 3 * rank // n_chip
    down = adapter_down[0]
    up = adapter_up[0]
    piece = width // (n_seg * n_chip)
    dma = pltpu.SemaphoreType.DMA
    any_space = pl.BlockSpec(memory_space=pl.ANY)
    smem = pl.BlockSpec(memory_space=pltpu.SMEM)
    exchange = [
        pltpu.VMEM((n_x, n_seg, rank, block), BF16),
        pltpu.VMEM((n_x, n_seg, half, block), BF16),
        pltpu.VMEM((n_seg, n_x, half, block), BF16),
        pltpu.VMEM((n_seg, half, block), BF16),
        pltpu.VMEM((n_x, half, block), BF16),
        pltpu.VMEM((n_seg, half, block), BF16),
        pltpu.VMEM((n_x, half, block), BF16),
    ]
    scratch = [
        pltpu.VMEM((tokens, width), BF16),
        pltpu.VMEM((tokens, width), BF16),
        pltpu.VMEM((rank, width), BF16),
        pltpu.VMEM((width, rank), BF16),
        pltpu.VMEM((tokens, rank), F32),
        pltpu.VMEM((n_seg, piece, rank), BF16),
        pltpu.VMEM((n_seg, rank, piece), BF16),
        pltpu.VMEM((piece, 3 * rank), BF16),
        pltpu.VMEM((n_chip, e_rows, rank), F32),
        pltpu.VMEM((n_chip, e_rows, rank), F32),
        pltpu.VMEM((n_seg, e_rows, rank), F32),
        pltpu.VMEM((2, n_chip, e_rows, rank), F32),
        pltpu.VMEM((n_seg, tokens, rank), BF16),
        pltpu.VMEM((n_seg, tokens, rank), BF16),
        pltpu.VMEM((2, tokens, 3 * rank), BF16),
        pltpu.VMEM((2, tokens, 4 * rank), BF16),
        pltpu.VMEM((n_x, block, 3 * rank), BF16),
        pltpu.VMEM((2, tokens, cols), BF16),
        pltpu.VMEM((2 * tokens, 128), F32),
        pltpu.VMEM((2 * tokens, 128), F32),
        pltpu.VMEM((2, 4 * rank, tokens), BF16),
        pltpu.VMEM((4 * rank, 3 * rank), BF16),
        *exchange,
        pltpu.VMEM((n_x, n_seg, rank, block), BF16),
        pltpu.VMEM((8, 128), F32),
        pltpu.VMEM((n_chip, 8, 128), F32),
        pltpu.VMEM((8, 128), F32),
        pltpu.VMEM((2 * n_seg, 8, 128), F32),
        *exchange,
        dma((chunks,)), dma((chunks,)), dma, dma, dma((2 + n_x,)),
        dma((n_seg,)), dma((n_seg,)), dma((n_seg,)), dma((n_seg,)),
        dma((n_chip,)), dma((n_chip,)), dma((n_seg,)), dma((n_seg,)), dma((n_chip,)), dma((n_chip,)), dma, dma,
        dma((n_seg,)), dma((n_seg,)), dma((n_seg,)), dma((n_seg,)),
        dma((n_chip,)), dma((n_chip,)), dma((n_x,)), dma((n_x,)),
        dma((n_seg,)), dma((n_seg,)), dma((n_seg,)), dma((n_seg,)),
        dma((4, n_seg)), dma((4, n_seg)), dma((4, n_seg)), dma((4, n_seg)),
        dma((n_chip,)), dma((n_chip,)), dma((2 * n_seg,)), dma((2 * n_seg,)),
        dma((4, n_seg)), dma((4, n_seg)),
    ]
    weights, grad = pl.pallas_call(
        kernel,
        out_shape=(
            jax.ShapeDtypeStruct((DOMAINS - 1,), F32),
            jax.ShapeDtypeStruct((rank, block), F32),
        ),
        in_specs=[any_space] * 4 + [smem, smem],
        out_specs=(smem, pl.BlockSpec(memory_space=pltpu.VMEM)),
        scratch_shapes=scratch,
        compiler_params=pltpu.CompilerParams(
            collective_id=0, has_side_effects=True, vmem_limit_bytes=56 * 1024 * 1024
        ),
    )(inputs, cotangent, down, up, domain_ids, prior_weights)
    return weights, grad[None]


def solution(mesh):
    return jax.shard_map(
        functools.partial(local, mesh.shape["dp"]),
        mesh=mesh,
        in_specs=(
            P("dp", None),
            P("dp", None),
            P("segment", None, None),
            P("segment", None, None),
            P(),
            P(),
        ),
        out_specs=(P(), P("segment", None, "dp")),
        check_vma=False,
    )
```

```python
import functools
import math

import jax
import jax.numpy as jnp
from jax import lax
from jax.experimental import pallas as pl
from jax.experimental.pallas import tpu as pltpu
from jax.sharding import PartitionSpec as P

DOMAINS = 9
TOK_MICRO = 56
SMOOTHING = 0.5
MESH = pl.DeviceIdType.MESH
F32 = jnp.float32
BF16 = jnp.bfloat16
NT = (((1,), (1,)), ((), ()))
NN = (((1,), (0,)), ((), ()))
TN = (((0,), (0,)), ((), ()))


def dot(a, b, dims):
    return lax.dot_general(a, b, dims, preferred_element_type=F32)


def remote(src, dst, send, recv, seg, dp):
    return pltpu.make_async_remote_copy(
        src_ref=src, dst_ref=dst, send_sem=send, recv_sem=recv, device_id=(seg, dp), device_id_type=MESH
    )


def all_in(ref, sem):
    pltpu.make_async_copy(ref, ref, sem).wait()


def each(lo, hi, body):
    def step(i, carry):
        body(i)
        return carry

    lax.fori_loop(lo, hi, step, 0)


def kernel(
    x_hbm, cot_hbm, down_hbm, up_hbm, ids_hbm, prior_hbm,
    wout_hbm, rout_hbm,
    ids, prior, wout, rout,
    xv, cv, dv, uv, acc, e_up, e_dn, e_cat, e_part, e_rs, e_seg, e_all, a_all, b_all, act_cat, inner_cat, inner_t,
    up_cat, xs, hot, row_w, lhs_t, cross,
    g_send, g_ra, g_rb, g_sa, g_sb, g_ra2, g_rb2, g_all, sc0, sc1, sc1s, sc2,
    f_send, f_ra, f_rb, f_sa, f_sb, f_ra2, f_rb2,
    s_x, s_c, s_d, s_u, s_loc, s_small,
    eu_s, eu_r, ed_s, ed_r, er_s, er_r, ey_s, ey_r, ea_s, ea_r, ep_s, ep_r,
    a_s, a_r, b_s, b_r, ue_s, ue_r, xp_s, xp_r, ac_s, ac_r, in_s, in_r, it_s, it_r,
    g_s, g_r, h_s, h_r, p_s, p_r, q_s, q_r, f_s, f_r,
):
    n_seg = 4
    n_chip = e_part.shape[0]
    n_x = n_chip // n_seg
    tokens, width = x_hbm.shape
    rank = down_hbm.shape[0]
    block = width // (2 * n_chip)
    cols = n_x * block
    chunks = 8
    kc = width // chunks
    half = rank // 2
    low, high = pl.ds(0, half), pl.ds(half, half)
    piece = width // (n_seg * n_chip)
    per = block // piece

    r = lax.axis_index("segment")
    dp = lax.axis_index("dp")
    c = dp % 2
    k = dp // 2
    z = k // n_x
    xx = k % n_x
    oc = 1 - c
    partner = k * 2 + oc
    up_core = (k // per) % 2

    def chip(n):
        return n * 2 + c

    def x_peer(i):
        return (xx + i) % n_x

    def z_peer(i):
        return (z + i) % n_seg

    bar = pltpu.get_barrier_semaphore()

    def greet(seg, d):
        pl.semaphore_signal(bar, inc=1, device_id=(seg, d), device_id_type=MESH)

    def greet_plane(i):
        greet(r, chip((k + i) % n_chip))

    each(1, n_chip, greet_plane)

    def greet_seg(i):
        greet((r + i) % n_seg, dp)
        greet((r + i) % n_seg, partner)

    each(1, n_seg, greet_seg)
    greet(r, partner)

    not_diag = z != r
    for i in range(n_seg):
        j = (z + i) % n_seg
        if i == 0:
            @pl.when(not_diag)
            def _():
                greet(z, chip(r * n_x + xx))
                greet(z, chip(r * n_x + xx))
        else:
            greet(j, chip(r * n_x + xx))
        j = (r + i) % n_seg
        if i == 0:
            @pl.when(not_diag)
            def _():
                greet(z, chip(r * n_x + xx))
                greet(z, chip(r * n_x + xx))
        else:
            greet(z, chip(j * n_x + xx))
    for i in range(1, n_x):
        j = (xx + i) % n_x
        greet(z, chip(r * n_x + j))
        greet(z, chip(r * n_x + j))

    def piece_of(seg):
        return pl.ds(pl.multiple_of((seg * n_chip + k) * piece, 128), piece)

    def own_dn():
        return pltpu.make_async_copy(down_hbm.at[:, piece_of(r)], e_dn.at[r], s_loc.at[0])

    def own_up():
        return pltpu.make_async_copy(up_hbm.at[piece_of(r), :], e_up.at[r], s_loc.at[1])

    def small(src, dst, i):
        return pltpu.make_async_copy(src, dst, s_small.at[i])

    small(ids_hbm, ids, 0).start()
    small(prior_hbm, prior, 1).start()
    own_dn().start()
    own_up().start()
    pltpu.make_async_copy(down_hbm, dv, s_d).start()

    x_copy = pltpu.make_async_copy(x_hbm, xv, s_x)
    c_copy = pltpu.make_async_copy(cot_hbm, cv, s_c)
    x_copy.start()
    pltpu.make_async_copy(up_hbm, uv, s_u).start()
    c_copy.start()

    def own_cols(i, core):
        return pl.ds(((r * n_x + i) * 2 + core) * block, block)

    def xe_copy(i):
        return pltpu.make_async_copy(
            x_hbm.at[:, own_cols(i, c)], xs.at[c, :, pl.ds(i * block, block)], s_loc.at[2]
        )

    each(0, n_x, lambda i: xe_copy(i).start())

    lane = lax.broadcasted_iota(jnp.int32, (1, 128), 1)

    def count(i, total):
        return total + jnp.where(lane == ids[i], 1.0, 0.0)

    small(ids_hbm, ids, 0).wait()
    small(prior_hbm, prior, 1).wait()
    counts = lax.fori_loop(0, ids.shape[0], count, jnp.zeros((1, 128), F32))
    scale = 1.0 / (counts * TOK_MICRO)
    micros = 2 * tokens // TOK_MICRO

    def fill(m):
        name = ids[k * micros + m]
        row = jnp.where(lane == name, scale, 0.0)
        hot[pl.ds(pl.multiple_of(m * TOK_MICRO, 8), TOK_MICRO), :] = jnp.broadcast_to(row, (TOK_MICRO, 128))

    each(0, micros, fill)

    def set_rows(weights):
        for h in range(2):
            row_w[h] = lax.dot_general(
                weights,
                hot[h * tokens:(h + 1) * tokens, :],
                NT,
                precision=lax.Precision.HIGHEST,
                preferred_element_type=F32,
            )

    lane8 = lax.broadcasted_iota(jnp.int32, (8, 128), 1)
    gen_scale = jnp.sum(jnp.where(lane == DOMAINS - 1, scale, 0.0), axis=1, keepdims=True)
    set_rows(jnp.where(lane8 == DOMAINS - 1, 1.0, 0.0))
    for h in range(2):
        row_w[h] = jnp.where(row_w[h] > 0.0, 1.0, 0.0)

    pl.semaphore_wait(bar, (n_chip - 1) + 2 * (n_seg - 1) + 1 + 2 * (n_seg + n_x) - jnp.where(not_diag, 0, 4))

    def e_up_from(j):
        return (j < n_seg - 1) & ((c == 0) & (j == 0) | (c == 1) & (j >= 1) | (c == up_core))

    def e_dn_from(j):
        return j >= 1 + c

    def e_up_copy(slot, peer):
        return remote(up_hbm.at[piece_of(peer), :], e_up.at[slot], eu_s.at[peer], eu_r.at[slot], peer, dp)

    def e_dn_copy(slot, peer):
        return remote(down_hbm.at[:, piece_of(peer)], e_dn.at[slot], ed_s.at[peer], ed_r.at[slot], peer, dp)

    for i in range(1, n_seg):
        peer = (r + i) % n_seg

        @pl.when(e_up_from(r))
        def _():
            e_up_copy(r, peer).start()

        @pl.when(e_dn_from(r))
        def _():
            e_dn_copy(r, peer).start()

    def xp_copy(i, slot_core, col_core):
        return remote(
            x_hbm.at[:, own_cols(i, col_core)],
            xs.at[slot_core, :, pl.ds(i * block, block)],
            xp_s,
            xp_r,
            r,
            partner,
        )

    each(0, n_x, lambda i: xp_copy(i, c, oc).start())

    pltpu.make_async_copy(down_hbm, dv, s_d).wait()
    acc[...] = jnp.zeros_like(acc)
    x_copy.wait()

    def a_step(i):
        sl = pl.ds(pl.multiple_of(i * kc, 128), kc)
        acc[...] += dot(xv[:, sl], dv[:, sl], NT)

    each(0, chunks, a_step)
    a_all[r] = acc[...]

    def seg_copy(buf, send, recv, slot, peer):
        return remote(buf.at[slot], buf.at[slot], send, recv, peer, dp)

    for i in range(1, n_seg):
        seg_copy(a_all, a_s, a_r, r, (r + i) % n_seg).start()

    three = pl.ds(0, n_seg - 1)
    others = pl.ds(0, n_chip - 1)

    for j in range(n_seg):
        @pl.when((j != r) & e_up_from(j))
        def _():
            e_up_copy(j, (r + 1) % n_seg).wait_recv()

        @pl.when((j != r) & e_dn_from(j))
        def _():
            e_dn_copy(j, (r + 1) % n_seg).wait_recv()

    own_dn().wait()
    own_up().wait()
    e_rows = e_part.shape[1]
    e_mats = []
    for m, (da, ua) in enumerate(((2, 1), (3, 1), (3, 2))):
        e_mats.append(dot(e_dn[(1 - c) * (m + 1) + c * da], e_up[c * ua], NN))
    e_part[...] = jnp.concatenate(e_mats, axis=0).reshape(n_chip, e_rows, rank)

    def er_copy(slot, n):
        return remote(e_part.at[n], e_rs.at[slot], er_s, er_r, r, chip(n))

    each(1, n_chip, lambda i: er_copy(k, (k + i) % n_chip).start())

    def up_slot(n):
        return up_cat.at[pl.ds(pl.multiple_of((n // (2 * per)) * block + (n % per) * piece, 128), piece)]

    def ue_copy(slot, n):
        return remote(e_cat, up_slot(slot), ue_s, ue_r, r, chip(n))

    @pl.when(c == up_core)
    def _():
        for j in range(n_seg - 1):
            e_cat[:, j * rank:(j + 1) * rank] = e_up[j]
        each(1, n_chip, lambda i: ue_copy(k, (k + i) % n_chip).start())
        up_slot(k)[...] = e_cat[...]

    pltpu.make_async_copy(up_hbm, uv, s_u).wait()
    acc[...] = jnp.zeros_like(acc)
    c_copy.wait()

    def b_step(i):
        sl = pl.ds(pl.multiple_of(i * kc, 128), kc)
        acc[...] += dot(cv[:, sl], uv[sl, :], NN)

    each(0, chunks, b_step)
    b_all[r] = acc[...]
    for i in range(1, n_seg):
        seg_copy(b_all, b_s, b_r, r, (r + i) % n_seg).start()

    e_rs[k] = e_part[k]
    all_in(e_rs.at[others], er_r)
    total = e_rs[0]
    for n in range(1, n_chip):
        total = total + e_rs[n]
    e_seg[r] = total
    for i in range(1, n_seg):
        seg_copy(e_seg, ey_s, ey_r, r, (r + i) % n_seg).start()
    all_in(e_seg.at[three], ey_r)
    e_all[c, k] = e_seg[0] + e_seg[1] + e_seg[2] + e_seg[3]

    def ea_copy(slot, n):
        return remote(e_all.at[c, slot], e_all.at[c, slot], ea_s, ea_r, r, chip(n))

    each(1, n_chip, lambda i: ea_copy(k, (k + i) % n_chip).start())

    all_in(e_all.at[c, others], ea_r)

    def ep_copy(core):
        return remote(e_all.at[core], e_all.at[core], ep_s, ep_r, r, partner)

    ep_copy(c).start()
    ep_copy(oc).wait_recv()

    all_in(a_all.at[three], a_r)

    def two_terms(m):
        high_part = m.astype(BF16)
        return high_part, (m - high_part.astype(F32)).astype(BF16)

    lower = {}
    for core, pairs in ((0, ((1, 0), (2, 0), (3, 0))), (1, ((2, 1), (3, 1), (3, 2)))):
        mats = e_all[core].reshape(3 * rank, rank)
        for m, pair in enumerate(pairs):
            lower[pair] = two_terms(mats[m * rank:(m + 1) * rank])

    def act_copy(j, core):
        ref = act_cat.at[core, :, pl.ds(j * rank, rank)]
        return remote(ref, ref, ac_s, ac_r, r, partner)

    def in_copy(core):
        return remote(inner_cat.at[core], inner_cat.at[core], in_s, in_r, r, partner)

    def it_copy(j, core):
        ref = inner_t.at[core, pl.ds(j * rank, rank)]
        return remote(ref, ref, it_s, it_r, r, partner)

    slopes = []
    acts = []
    for s in range(n_seg):
        pre = a_all[s]
        for j in range(s):
            pre = pre + dot(acts[j], lower[(s, j)][0], NT) + dot(acts[j], lower[(s, j)][1], NT)
        sig = 1.0 / (1.0 + jnp.exp(-pre))
        slopes.append(sig * (1.0 + pre * (1.0 - sig)))
        if s < n_seg - 1:
            act = (pre * sig).astype(BF16)
            acts.append(act)
            act_cat[c, :, s * rank:(s + 1) * rank] = act
            act_copy(s, c).start()

    all_in(b_all.at[three], b_r)

    inners = [None] * n_seg
    for s in reversed(range(n_seg)):
        pulled = b_all[s]
        for j in range(s + 1, n_seg):
            pulled = pulled + dot(inners[j], lower[(j, s)][0], NN) + dot(inners[j], lower[(j, s)][1], NN)
        wide = pulled * slopes[s]
        inner = wide.astype(BF16)
        inners[s] = inner
        inner_t[c, s * rank:(s + 1) * rank, :] = wide.T.astype(BF16)
        it_copy(s, c).start()
        inner_cat[c, :, s * rank:(s + 1) * rank] = inner

    in_copy(c).start()

    all_in(xs.at[c], s_loc.at[2])
    all_in(xs.at[oc], xp_r)

    @pl.when(c == up_core)
    def _():
        all_in(up_cat.at[pl.ds(0, n_x * block - piece)], ue_r)

    @pl.when(c != up_core)
    def _():
        all_in(up_cat, ue_r)

    all_in(act_cat.at[oc], ac_r)
    all_in(inner_t.at[oc], it_r)
    stack = n_seg * rank
    lower_mask = (
        lax.broadcasted_iota(jnp.int32, (stack, stack - rank), 0) // rank
        > lax.broadcasted_iota(jnp.int32, (stack, stack - rank), 1) // rank
    )

    def set_weighted():
        for h in range(2):
            weight = row_w[h, 0:1, :]
            for s in range(n_seg):
                rows = slice(s * rank, (s + 1) * rank)
                lhs_t[h, rows, :] = (inner_t[h, rows, :].astype(F32) * weight).astype(BF16)
        both = dot(lhs_t[0], act_cat[0], NN) + dot(lhs_t[1], act_cat[1], NN)
        cross[...] = jnp.where(lower_mask, both, 0.0).astype(BF16)

    def weighted_grad(i):
        sl = pl.ds(pl.multiple_of(i * block, 128), block)
        total = dot(lhs_t[0], xs[0, :, sl], NN) + dot(lhs_t[1], xs[1, :, sl], NN)
        return total + dot(cross[...], up_cat[pl.ds(pl.multiple_of(i * block, 128), block), :], NT)

    def first_a(send, recv, ss, rs, slot, i):
        return remote(send.at[i, :, low], recv.at[slot], ss.at[0], rs.at[0], r, chip(z * n_x + i))

    def first_b(send, recv, ss, rs, slot, j):
        return remote(send.at[:, j, high], recv.at[slot], ss.at[1], rs.at[1], r, chip(j * n_x + xx))

    def spread(send, recv_a, recv_b, ss, rs, factor):
        set_weighted()

        def column_block(t):
            i = (xx + 1 + t) % n_x
            send[i] = (weighted_grad(i) * factor).reshape(n_seg, rank, block).astype(BF16)

            @pl.when(i != xx)
            def _():
                first_a(send, recv_a, ss, rs, xx, i).start()

        each(0, n_x, column_block)
        for t in range(1, n_seg):
            first_b(send, recv_b, ss, rs, z, z_peer(t)).start()

    def pick(count):
        return pl.ds(0, count - 1)

    def join(ref, sem, axis_len):
        if axis_len > 1:
            all_in(ref, sem)

    def total_of(ref, count):
        total = ref[0].astype(F32)
        for i in range(1, count):
            total = total + ref[i].astype(F32)
        return total

    def sum_a(send, recv_a, rs):
        recv_a[xx] = send[xx, :, :half]
        join(recv_a.at[pick(n_x)], rs.at[0], n_x)
        return total_of(recv_a, n_x).astype(BF16)

    def sum_b(send, recv_b, rs):
        recv_b[z] = send[:, z, half:]
        join(recv_b.at[pick(n_seg)], rs.at[1], n_seg)
        return total_of(recv_b, n_seg).astype(BF16)

    spread(g_send, g_ra, g_rb, g_s, g_r, gen_scale)
    g_sa[...] = sum_a(g_send, g_ra, g_r)

    def second_a(slot, j):
        return remote(g_sa.at[j], g_ra2.at[slot], g_s.at[2], g_r.at[2], r, chip(j * n_x + xx))

    def second_b(slot, i):
        return remote(g_sb.at[i], g_rb2.at[slot], g_s.at[3], g_r.at[3], r, chip(z * n_x + i))

    for t in range(1, n_seg):
        second_a(z, z_peer(t)).start()
    g_sb[...] = sum_b(g_send, g_rb, g_r)
    for t in range(1, n_x):
        second_b(xx, x_peer(t)).start()
    g_ra2[z] = g_sa[z]
    join(g_ra2.at[pick(n_seg)], g_r.at[2], n_seg)
    total = total_of(g_ra2, n_seg)
    g_all[xx, z, :half] = total.astype(BF16)

    def gather(stage, slot, i, j):
        if stage == 0:
            ref, to = g_all.at[slot, z, low], z * n_x + i
        elif stage == 1:
            ref, to = g_all.at[xx, slot, high], j * n_x + xx
        elif stage == 2:
            ref, to = g_all.at[:, slot, low], j * n_x + xx
        else:
            ref, to = g_all.at[slot, :, high], z * n_x + i
        return remote(ref, ref, h_s.at[stage], h_r.at[stage], r, chip(to))

    for t in range(1, n_x):
        gather(0, xx, x_peer(t), z).start()
    g_rb2[xx] = g_sb[xx]
    join(g_rb2.at[pick(n_x)], g_r.at[3], n_x)
    total = total_of(g_rb2, n_x)
    g_all[xx, z, half:] = total.astype(BF16)
    for t in range(1, n_seg):
        gather(1, z, xx, z_peer(t)).start()

    join(g_all.at[pick(n_x), z, low], h_r.at[0], n_x)
    for t in range(1, n_seg):
        gather(2, z, xx, z_peer(t)).start()
    join(g_all.at[xx, pick(n_seg), high], h_r.at[1], n_seg)
    for t in range(1, n_x):
        gather(3, xx, x_peer(t), z).start()
    join(g_all.at[:, pick(n_seg), low], h_r.at[2], n_seg)

    y0 = jnp.zeros((tokens, stack), F32)
    y1 = jnp.zeros((tokens, stack), F32)
    gu = jnp.zeros((stack, stack - rank), F32)
    for t in range(n_x):
        i = x_peer(t)
        if t == 1:
            join(g_all.at[pick(n_x), :, high], h_r.at[3], n_x)
        grad = g_all[i].reshape(stack, block)
        sl = pl.ds(pl.multiple_of(i * block, 128), block)
        y0 = y0 + dot(xs[0, :, sl], grad, NT)
        y1 = y1 + dot(xs[1, :, sl], grad, NT)
        gu = gu + dot(grad, up_cat[sl, :], NN)
    gu = jnp.where(lower_mask, gu, 0.0).astype(BF16)
    in_copy(oc).wait_recv()
    mine = jnp.zeros((1, 128), F32)
    for h, y in ((0, y0), (1, y1)):
        y = (y + dot(act_cat[h], gu, NT)) * inner_cat[h].astype(F32)
        row = jnp.sum(y, axis=1, keepdims=True)
        mine = mine + jnp.sum(hot[h * tokens:(h + 1) * tokens, :] * row, axis=0, keepdims=True)
    sc0[...] = jnp.broadcast_to(mine, (8, 128))

    def p_copy(slot, n):
        return remote(sc0, sc1.at[slot], p_s, p_r, r, chip(n))

    for i in range(1, n_chip):
        p_copy(k, (k + i) % n_chip).start()

    sc1[k] = sc0[...]
    all_in(sc1.at[others], p_r)
    plane = total_of(sc1, n_chip)
    sc1s[...] = plane

    def q_copy(slot, n):
        return remote(sc1s, sc2.at[slot], q_s, q_r, n // 2, k * 2 + n % 2)

    here = r * 2 + c
    for i in range(1, 2 * n_seg):
        q_copy(here, (here + i) % (2 * n_seg)).start()

    sc2[here] = plane
    all_in(sc2.at[pl.ds(0, 2 * n_seg - 1)], q_r)
    scores = total_of(sc2, 2 * n_seg)

    entries = n_seg * rank * width
    mean_gen = jnp.sum(jnp.where(lane8 == DOMAINS - 1, scores, 0.0), axis=1, keepdims=True) / entries
    zed = scores / (math.sqrt(entries) * (mean_gen + 1e-06))
    prior_row = jnp.zeros((8, 128), F32)
    for i in range(DOMAINS - 1):
        prior_row = jnp.where(lane8 == i, prior[i], prior_row)
    train = lane8 < DOMAINS - 1
    raised = jnp.where(train, prior_row * jnp.exp(4.0 * jnp.tanh(zed / 4.0)), 0.0)
    weights = SMOOTHING / (DOMAINS - 1) + (1.0 - SMOOTHING) * raised / jnp.sum(raised, axis=1, keepdims=True)
    weights = jnp.where(train, weights, 0.0)
    set_rows(weights)

    spread(f_send, f_ra, f_rb, f_s, f_r, 1.0)
    for i in range(DOMAINS - 1):
        wout[i] = jnp.sum(jnp.where(lane == i, weights[0:1], 0.0))
    small(wout, wout_hbm, 0).start()

    def last_a(slot, s):
        return remote(f_sa.at[s], f_ra2.at[slot], f_s.at[2], f_r.at[2], s, chip(r * n_x + xx))

    def last_b(slot, i):
        return remote(f_sb.at[i], f_rb2.at[slot], f_s.at[3], f_r.at[3], z, chip(r * n_x + i))

    f_sa[...] = sum_a(f_send, f_ra, f_r)
    for t in range(1, n_seg):
        last_a(z, z_peer(t)).start()

    @pl.when(not_diag)
    def _():
        last_a(z, z).start()

    @pl.when(z == r)
    def _():
        f_ra2[z] = f_sa[z]

    f_sb[...] = sum_b(f_send, f_rb, f_r)
    for t in range(1, n_x):
        last_b(xx, x_peer(t)).start()

    @pl.when(not_diag)
    def _():
        last_b(xx, xx).start()

    @pl.when(z == r)
    def _():
        f_rb2[xx] = f_sb[xx]

    def join_last(ref, sem, count):
        @pl.when(not_diag)
        def _():
            all_in(ref, sem)

        @pl.when(z == r)
        def _():
            join(ref.at[pick(count)], sem, count)

    join_last(f_ra2, f_r.at[2], n_seg)
    rout[:half] = total_of(f_ra2, n_seg)
    small(rout.at[low], rout_hbm.at[low], 1).start()
    join_last(f_rb2, f_r.at[3], n_x)
    rout[half:] = total_of(f_rb2, n_x)
    small(rout.at[high], rout_hbm.at[high], 2).start()

    for i in range(1, n_seg):
        peer = (r + i) % n_seg

        @pl.when(e_up_from(r))
        def _():
            e_up_copy(r, peer).wait_send()

        @pl.when(e_dn_from(r))
        def _():
            e_dn_copy(r, peer).wait_send()


    all_in(a_all.at[three], a_s)
    all_in(b_all.at[three], b_s)
    all_in(e_seg.at[three], ey_s)
    all_in(xs.at[c], xp_s)
    ep_copy(c).wait_send()
    all_in(act_cat.at[c], ac_s)
    all_in(inner_t.at[c], it_s)
    in_copy(c).wait_send()
    all_in(e_part.at[others], er_s)
    all_in(e_all.at[c, others], ea_s)
    all_in(sc1.at[others], p_s)
    all_in(sc2.at[pl.ds(0, 2 * n_seg - 1)], q_s)

    @pl.when(c == up_core)
    def _():
        all_in(uv.at[pl.ds(0, (n_chip - 1) * piece * (n_seg - 1))], ue_s)

    for send, sems in ((g_send, g_s), (f_send, f_s)):
        join(send.at[pick(n_x), :, low], sems.at[0], n_x)
        join(send.at[:, pick(n_seg), high], sems.at[1], n_seg)
    join(g_sa.at[pick(n_seg)], g_s.at[2], n_seg)
    join(g_sb.at[pick(n_x)], g_s.at[3], n_x)
    join(g_all.at[pick(n_x), z, low], h_s.at[0], n_x)
    join(g_all.at[xx, pick(n_seg), high], h_s.at[1], n_seg)
    join(g_all.at[:, pick(n_seg), low], h_s.at[2], n_seg)
    join(g_all.at[pick(n_x), :, high], h_s.at[3], n_x)
    join_last(f_sa, f_s.at[2], n_seg)
    join_last(f_sb, f_s.at[3], n_x)
    small(wout, wout_hbm, 0).wait()
    small(rout.at[low], rout_hbm.at[low], 1).wait()
    small(rout.at[high], rout_hbm.at[high], 2).wait()


def local(n_dp, inputs, cotangent, adapter_down, adapter_up, domain_ids, prior_weights):
    n_seg = 4
    n_chip = n_dp // 2
    n_x = n_chip // n_seg
    tokens, width = inputs.shape
    rank = adapter_down.shape[1]
    block = width // n_dp
    cols = n_x * block
    half = rank // 2
    e_rows = 3 * rank // n_chip
    down = adapter_down[0]
    up = adapter_up[0]
    piece = width // (n_seg * n_chip)
    dma = pltpu.SemaphoreType.DMA
    any_space = pl.BlockSpec(memory_space=pl.ANY)
    exchange = [
        pltpu.VMEM((n_x, n_seg, rank, block), BF16),
        pltpu.VMEM((n_x, n_seg, half, block), BF16),
        pltpu.VMEM((n_seg, n_x, half, block), BF16),
        pltpu.VMEM((n_seg, half, block), BF16),
        pltpu.VMEM((n_x, half, block), BF16),
        pltpu.VMEM((n_seg, half, block), BF16),
        pltpu.VMEM((n_x, half, block), BF16),
    ]
    scratch = [
        pltpu.SMEM(domain_ids.shape, jnp.int32),
        pltpu.SMEM(prior_weights.shape, F32),
        pltpu.SMEM((DOMAINS - 1,), F32),
        pltpu.VMEM((rank, block), F32),
        pltpu.VMEM((tokens, width), BF16),
        pltpu.VMEM((tokens, width), BF16),
        pltpu.VMEM((rank, width), BF16),
        pltpu.VMEM((width, rank), BF16),
        pltpu.VMEM((tokens, rank), F32),
        pltpu.VMEM((n_seg, piece, rank), BF16),
        pltpu.VMEM((n_seg, rank, piece), BF16),
        pltpu.VMEM((piece, 3 * rank), BF16),
        pltpu.VMEM((n_chip, e_rows, rank), F32),
        pltpu.VMEM((n_chip, e_rows, rank), F32),
        pltpu.VMEM((n_seg, e_rows, rank), F32),
        pltpu.VMEM((2, n_chip, e_rows, rank), F32),
        pltpu.VMEM((n_seg, tokens, rank), F32),
        pltpu.VMEM((n_seg, tokens, rank), F32),
        pltpu.VMEM((2, tokens, 3 * rank), BF16),
        pltpu.VMEM((2, tokens, 4 * rank), BF16),
        pltpu.VMEM((2, 4 * rank, tokens), BF16),
        pltpu.VMEM((n_x * block, 3 * rank), BF16),
        pltpu.VMEM((2, tokens, cols), BF16),
        pltpu.VMEM((2 * tokens, 128), F32),
        pltpu.VMEM((2, 8, tokens), F32),
        pltpu.VMEM((2, 4 * rank, tokens), BF16),
        pltpu.VMEM((4 * rank, 3 * rank), BF16),
        *exchange,
        pltpu.VMEM((n_x, n_seg, rank, block), BF16),
        pltpu.VMEM((8, 128), F32),
        pltpu.VMEM((n_chip, 8, 128), F32),
        pltpu.VMEM((8, 128), F32),
        pltpu.VMEM((2 * n_seg, 8, 128), F32),
        *exchange,
        dma, dma, dma, dma, dma((3,)), dma((3,)),
        dma((n_seg,)), dma((n_seg,)), dma((n_seg,)), dma((n_seg,)),
        dma, dma, dma, dma, dma, dma, dma, dma,
        dma, dma, dma, dma, dma, dma, dma, dma,
        dma, dma, dma, dma, dma, dma,
        dma((4,)), dma((4,)), dma((4,)), dma((4,)),
        dma, dma, dma, dma,
        dma((4,)), dma((4,)),
    ]
    weights, grad = pl.pallas_call(
        kernel,
        out_shape=(
            jax.ShapeDtypeStruct((DOMAINS - 1,), F32),
            jax.ShapeDtypeStruct((rank, block), F32),
        ),
        in_specs=[any_space] * 6,
        out_specs=(any_space, any_space),
        scratch_shapes=scratch,
        compiler_params=pltpu.CompilerParams(
            collective_id=0, has_side_effects=True, vmem_limit_bytes=56 * 1024 * 1024
        ),
    )(inputs, cotangent, down, up, domain_ids, prior_weights)
    return weights, grad[None]


def solution(mesh):
    return jax.shard_map(
        functools.partial(local, mesh.shape["dp"]),
        mesh=mesh,
        in_specs=(
            P("dp", None),
            P("dp", None),
            P("segment", None, None),
            P("segment", None, None),
            P(),
            P(),
        ),
        out_specs=(P(), P("segment", None, "dp")),
        check_vma=False,
    )
```

```python
import functools
import math

import jax
import jax.numpy as jnp
from jax import lax
from jax.experimental import pallas as pl
from jax.experimental.pallas import tpu as pltpu
from jax.sharding import PartitionSpec as P

DOMAINS = 9
TOK_MICRO = 56
SMOOTHING = 0.5
MESH = pl.DeviceIdType.MESH
F32 = jnp.float32
BF16 = jnp.bfloat16
NT = (((1,), (1,)), ((), ()))
NN = (((1,), (0,)), ((), ()))
TN = (((0,), (0,)), ((), ()))


def dot(a, b, dims):
    return lax.dot_general(a, b, dims, preferred_element_type=F32)


def remote(src, dst, send, recv, seg, dp):
    return pltpu.make_async_remote_copy(
        src_ref=src, dst_ref=dst, send_sem=send, recv_sem=recv, device_id=(seg, dp), device_id_type=MESH
    )


def all_in(ref, sem):
    pltpu.make_async_copy(ref, ref, sem).wait()


def each(lo, hi, body):
    def step(i, carry):
        body(i)
        return carry

    lax.fori_loop(lo, hi, step, 0)


def kernel(
    x_hbm, cot_hbm, down_hbm, up_hbm, ids_hbm, prior_hbm,
    wout_hbm, rout_hbm,
    ids, prior, wout, rout,
    xv, cv, dv, uv, acc, e_up, e_dn, e_cat, e_part, e_rs, e_seg, e_all, a_all, b_all, act_cat, inner_cat, inner_t,
    up_cat, xs, hot, row_w, lhs_t, cross,
    g_send, g_ra, g_rb, g_sa, g_sb, g_ra2, g_rb2, g_all, sc0, sc1, sc1s, sc2,
    f_send, f_ra, f_rb, f_sa, f_sb, f_ra2, f_rb2,
    s_x, s_c, s_d, s_u, s_loc, s_small,
    eu_s, eu_r, ed_s, ed_r, er_s, er_r, ey_s, ey_r, ea_s, ea_r, ep_s, ep_r,
    a_s, a_r, b_s, b_r, ue_s, ue_r, xp_s, xp_r, ac_s, ac_r, in_s, in_r, it_s, it_r,
    g_s, g_r, h_s, h_r, p_s, p_r, q_s, q_r, f_s, f_r,
):
    n_seg = 4
    n_chip = e_part.shape[0]
    n_x = n_chip // n_seg
    tokens, width = x_hbm.shape
    rank = down_hbm.shape[0]
    block = width // (2 * n_chip)
    cols = n_x * block
    chunks = 8
    kc = width // chunks
    half = rank // 2
    low, high = pl.ds(0, half), pl.ds(half, half)
    piece = width // (n_seg * n_chip)
    per = block // piece

    r = lax.axis_index("segment")
    dp = lax.axis_index("dp")
    c = dp % 2
    k = dp // 2
    z = k // n_x
    xx = k % n_x
    oc = 1 - c
    partner = k * 2 + oc
    up_core = (k // per) % 2

    def chip(n):
        return n * 2 + c

    def x_peer(i):
        return (xx + i) % n_x

    def z_peer(i):
        return (z + i) % n_seg

    bar = pltpu.get_barrier_semaphore()

    def greet(seg, d):
        pl.semaphore_signal(bar, inc=1, device_id=(seg, d), device_id_type=MESH)

    def greet_plane(i):
        greet(r, chip((k + i) % n_chip))

    each(1, n_chip, greet_plane)

    def greet_seg(i):
        greet((r + i) % n_seg, dp)
        greet((r + i) % n_seg, partner)

    each(1, n_seg, greet_seg)
    greet(r, partner)

    not_diag = z != r
    for i in range(n_seg):
        j = (z + i) % n_seg
        if i == 0:
            @pl.when(not_diag)
            def _():
                greet(z, chip(r * n_x + xx))
                greet(z, chip(r * n_x + xx))
        else:
            greet(j, chip(r * n_x + xx))
        j = (r + i) % n_seg
        if i == 0:
            @pl.when(not_diag)
            def _():
                greet(z, chip(r * n_x + xx))
                greet(z, chip(r * n_x + xx))
        else:
            greet(z, chip(j * n_x + xx))
    for i in range(1, n_x):
        j = (xx + i) % n_x
        greet(z, chip(r * n_x + j))
        greet(z, chip(r * n_x + j))

    def piece_of(seg):
        return pl.ds(pl.multiple_of((seg * n_chip + k) * piece, 128), piece)

    def own_dn():
        return pltpu.make_async_copy(down_hbm.at[:, piece_of(r)], e_dn.at[r], s_loc.at[0])

    def own_up():
        return pltpu.make_async_copy(up_hbm.at[piece_of(r), :], e_up.at[r], s_loc.at[1])

    def small(src, dst, i):
        return pltpu.make_async_copy(src, dst, s_small.at[i])

    small(ids_hbm, ids, 0).start()
    small(prior_hbm, prior, 1).start()
    own_dn().start()
    own_up().start()
    pltpu.make_async_copy(down_hbm, dv, s_d).start()

    x_copy = pltpu.make_async_copy(x_hbm, xv, s_x)
    c_copy = pltpu.make_async_copy(cot_hbm, cv, s_c)
    x_copy.start()
    pltpu.make_async_copy(up_hbm, uv, s_u).start()
    c_copy.start()

    def own_cols(i, core):
        return pl.ds(((r * n_x + i) * 2 + core) * block, block)

    def xe_copy(i):
        return pltpu.make_async_copy(
            x_hbm.at[:, own_cols(i, c)], xs.at[c, :, pl.ds(i * block, block)], s_loc.at[2]
        )

    each(0, n_x, lambda i: xe_copy(i).start())

    lane = lax.broadcasted_iota(jnp.int32, (1, 128), 1)

    def count(i, total):
        return total + jnp.where(lane == ids[i], 1.0, 0.0)

    small(ids_hbm, ids, 0).wait()
    small(prior_hbm, prior, 1).wait()
    counts = lax.fori_loop(0, ids.shape[0], count, jnp.zeros((1, 128), F32))
    scale = 1.0 / (counts * TOK_MICRO)
    micros = 2 * tokens // TOK_MICRO

    def fill(m):
        name = ids[k * micros + m]
        row = jnp.where(lane == name, scale, 0.0)
        hot[pl.ds(pl.multiple_of(m * TOK_MICRO, 8), TOK_MICRO), :] = jnp.broadcast_to(row, (TOK_MICRO, 128))

    each(0, micros, fill)

    def set_rows(weights):
        for h in range(2):
            row_w[h] = lax.dot_general(
                weights,
                hot[h * tokens:(h + 1) * tokens, :],
                NT,
                precision=lax.Precision.HIGHEST,
                preferred_element_type=F32,
            )

    lane8 = lax.broadcasted_iota(jnp.int32, (8, 128), 1)
    gen_scale = jnp.sum(jnp.where(lane == DOMAINS - 1, scale, 0.0), axis=1, keepdims=True)
    set_rows(jnp.where(lane8 == DOMAINS - 1, 1.0, 0.0))
    for h in range(2):
        row_w[h] = jnp.where(row_w[h] > 0.0, 1.0, 0.0)

    pl.semaphore_wait(bar, (n_chip - 1) + 2 * (n_seg - 1) + 1 + 2 * (n_seg + n_x) - jnp.where(not_diag, 0, 4))

    def e_up_from(j):
        return (j < n_seg - 1) & ((c == 0) & (j == 0) | (c == 1) & (j >= 1) | (c == up_core))

    def e_dn_from(j):
        return j >= 1 + c

    def e_up_copy(slot, peer):
        return remote(up_hbm.at[piece_of(peer), :], e_up.at[slot], eu_s.at[peer], eu_r.at[slot], peer, dp)

    def e_dn_copy(slot, peer):
        return remote(down_hbm.at[:, piece_of(peer)], e_dn.at[slot], ed_s.at[peer], ed_r.at[slot], peer, dp)

    for i in range(1, n_seg):
        peer = (r + i) % n_seg

        @pl.when(e_up_from(r))
        def _():
            e_up_copy(r, peer).start()

        @pl.when(e_dn_from(r))
        def _():
            e_dn_copy(r, peer).start()

    def xp_copy(i, slot_core, col_core):
        return remote(
            x_hbm.at[:, own_cols(i, col_core)],
            xs.at[slot_core, :, pl.ds(i * block, block)],
            xp_s,
            xp_r,
            r,
            partner,
        )

    each(0, n_x, lambda i: xp_copy(i, c, oc).start())

    pltpu.make_async_copy(down_hbm, dv, s_d).wait()
    acc[...] = jnp.zeros_like(acc)
    x_copy.wait()

    def a_step(i):
        sl = pl.ds(pl.multiple_of(i * kc, 128), kc)
        acc[...] += dot(xv[:, sl], dv[:, sl], NT)

    each(0, chunks, a_step)
    a_all[r] = acc[...]

    def seg_copy(buf, send, recv, slot, peer):
        return remote(buf.at[slot], buf.at[slot], send, recv, peer, dp)


    behind, ahead = (r + n_seg - 1) % n_seg, (r + 1) % n_seg
    first_rows, last_rows = pl.ds(0, tokens // 2), pl.ds(tokens // 2, tokens // 2)

    def near(buf, send, recv):
        remote(buf.at[r], buf.at[r], send.at[0], recv.at[0], ahead, dp).start()
        remote(buf.at[r], buf.at[r], send.at[0], recv.at[0], behind, dp).start()

    def pass_on(buf, send, recv):
        all_in(buf.at[pl.ds(0, 2)], recv.at[0])
        up_ref = buf.at[behind, first_rows]
        down_ref = buf.at[ahead, last_rows]
        remote(up_ref, up_ref, send.at[1], recv.at[1], ahead, dp).start()
        remote(down_ref, down_ref, send.at[1], recv.at[1], behind, dp).start()

    near(a_all, a_s, a_r)

    three = pl.ds(0, n_seg - 1)
    others = pl.ds(0, n_chip - 1)

    for j in range(n_seg):
        @pl.when((j != r) & e_up_from(j))
        def _():
            e_up_copy(j, (r + 1) % n_seg).wait_recv()

        @pl.when((j != r) & e_dn_from(j))
        def _():
            e_dn_copy(j, (r + 1) % n_seg).wait_recv()

    own_dn().wait()
    own_up().wait()
    e_rows = e_part.shape[1]
    e_mats = []
    for m, (da, ua) in enumerate(((2, 1), (3, 1), (3, 2))):
        e_mats.append(dot(e_dn[(1 - c) * (m + 1) + c * da], e_up[c * ua], NN))
    e_part[...] = jnp.concatenate(e_mats, axis=0).reshape(n_chip, e_rows, rank)

    def er_copy(slot, n):
        return remote(e_part.at[n], e_rs.at[slot], er_s, er_r, r, chip(n))

    each(1, n_chip, lambda i: er_copy(k, (k + i) % n_chip).start())

    def up_slot(n):
        return up_cat.at[pl.ds(pl.multiple_of((n // (2 * per)) * block + (n % per) * piece, 128), piece)]

    def ue_copy(slot, n):
        return remote(e_cat, up_slot(slot), ue_s, ue_r, r, chip(n))

    @pl.when(c == up_core)
    def _():
        for j in range(n_seg - 1):
            e_cat[:, j * rank:(j + 1) * rank] = e_up[j]
        each(1, n_chip, lambda i: ue_copy(k, (k + i) % n_chip).start())
        up_slot(k)[...] = e_cat[...]

    pltpu.make_async_copy(up_hbm, uv, s_u).wait()
    acc[...] = jnp.zeros_like(acc)
    c_copy.wait()

    def b_step(i):
        sl = pl.ds(pl.multiple_of(i * kc, 128), kc)
        acc[...] += dot(cv[:, sl], uv[sl, :], NN)

    each(0, chunks, b_step)
    b_all[r] = acc[...]
    near(b_all, b_s, b_r)

    e_rs[k] = e_part[k]
    all_in(e_rs.at[others], er_r)
    total = e_rs[0]
    for n in range(1, n_chip):
        total = total + e_rs[n]
    e_seg[r] = total
    for i in range(1, n_seg):
        seg_copy(e_seg, ey_s, ey_r, r, (r + i) % n_seg).start()
    all_in(e_seg.at[three], ey_r)
    e_all[c, k] = e_seg[0] + e_seg[1] + e_seg[2] + e_seg[3]

    def ea_copy(slot, n):
        return remote(e_all.at[c, slot], e_all.at[c, slot], ea_s, ea_r, r, chip(n))

    each(1, n_chip, lambda i: ea_copy(k, (k + i) % n_chip).start())

    pass_on(a_all, a_s, a_r)

    all_in(e_all.at[c, others], ea_r)

    def ep_copy(core):
        return remote(e_all.at[core], e_all.at[core], ep_s, ep_r, r, partner)

    ep_copy(c).start()
    ep_copy(oc).wait_recv()

    pass_on(b_all, b_s, b_r)
    all_in(a_all.at[0], a_r.at[1])

    def two_terms(m):
        high_part = m.astype(BF16)
        return high_part, (m - high_part.astype(F32)).astype(BF16)

    lower = {}
    for core, pairs in ((0, ((1, 0), (2, 0), (3, 0))), (1, ((2, 1), (3, 1), (3, 2)))):
        mats = e_all[core].reshape(3 * rank, rank)
        for m, pair in enumerate(pairs):
            lower[pair] = two_terms(mats[m * rank:(m + 1) * rank])

    def act_copy(j, core):
        ref = act_cat.at[core, :, pl.ds(j * rank, rank)]
        return remote(ref, ref, ac_s, ac_r, r, partner)

    def in_copy(core):
        return remote(inner_cat.at[core], inner_cat.at[core], in_s, in_r, r, partner)

    def it_copy(j, core):
        ref = inner_t.at[core, pl.ds(j * rank, rank)]
        return remote(ref, ref, it_s, it_r, r, partner)

    slopes = []
    acts = []
    for s in range(n_seg):
        pre = a_all[s]
        for j in range(s):
            pre = pre + dot(acts[j], lower[(s, j)][0], NT) + dot(acts[j], lower[(s, j)][1], NT)
        sig = 1.0 / (1.0 + jnp.exp(-pre))
        slopes.append(sig * (1.0 + pre * (1.0 - sig)))
        if s < n_seg - 1:
            act = (pre * sig).astype(BF16)
            acts.append(act)
            act_cat[c, :, s * rank:(s + 1) * rank] = act
            act_copy(s, c).start()

    all_in(b_all.at[0], b_r.at[1])

    inners = [None] * n_seg
    for s in reversed(range(n_seg)):
        pulled = b_all[s]
        for j in range(s + 1, n_seg):
            pulled = pulled + dot(inners[j], lower[(j, s)][0], NN) + dot(inners[j], lower[(j, s)][1], NN)
        wide = pulled * slopes[s]
        inner = wide.astype(BF16)
        inners[s] = inner
        inner_t[c, s * rank:(s + 1) * rank, :] = wide.T.astype(BF16)
        it_copy(s, c).start()
        inner_cat[c, :, s * rank:(s + 1) * rank] = inner

    in_copy(c).start()

    all_in(xs.at[c], s_loc.at[2])
    all_in(xs.at[oc], xp_r)

    @pl.when(c == up_core)
    def _():
        all_in(up_cat.at[pl.ds(0, n_x * block - piece)], ue_r)

    @pl.when(c != up_core)
    def _():
        all_in(up_cat, ue_r)

    all_in(act_cat.at[oc], ac_r)
    all_in(inner_t.at[oc], it_r)
    stack = n_seg * rank
    lower_mask = (
        lax.broadcasted_iota(jnp.int32, (stack, stack - rank), 0) // rank
        > lax.broadcasted_iota(jnp.int32, (stack, stack - rank), 1) // rank
    )

    def set_weighted():
        for h in range(2):
            weight = row_w[h, 0:1, :]
            for s in range(n_seg):
                rows = slice(s * rank, (s + 1) * rank)
                lhs_t[h, rows, :] = (inner_t[h, rows, :].astype(F32) * weight).astype(BF16)
        both = dot(lhs_t[0], act_cat[0], NN) + dot(lhs_t[1], act_cat[1], NN)
        cross[...] = jnp.where(lower_mask, both, 0.0).astype(BF16)

    def weighted_grad(i):
        sl = pl.ds(pl.multiple_of(i * block, 128), block)
        total = dot(lhs_t[0], xs[0, :, sl], NN) + dot(lhs_t[1], xs[1, :, sl], NN)
        return total + dot(cross[...], up_cat[pl.ds(pl.multiple_of(i * block, 128), block), :], NT)

    def first_a(send, recv, ss, rs, slot, i):
        return remote(send.at[i, :, low], recv.at[slot], ss.at[0], rs.at[0], r, chip(z * n_x + i))

    def first_b(send, recv, ss, rs, slot, j):
        return remote(send.at[:, j, high], recv.at[slot], ss.at[1], rs.at[1], r, chip(j * n_x + xx))

    def spread(send, recv_a, recv_b, ss, rs, factor):
        set_weighted()

        def column_block(t):
            i = (xx + 1 + t) % n_x
            send[i] = (weighted_grad(i) * factor).reshape(n_seg, rank, block).astype(BF16)

            @pl.when(i != xx)
            def _():
                first_a(send, recv_a, ss, rs, xx, i).start()

        each(0, n_x, column_block)
        for t in range(1, n_seg):
            first_b(send, recv_b, ss, rs, z, z_peer(t)).start()

    def pick(count):
        return pl.ds(0, count - 1)

    def join(ref, sem, axis_len):
        if axis_len > 1:
            all_in(ref, sem)

    def total_of(ref, count):
        total = ref[0].astype(F32)
        for i in range(1, count):
            total = total + ref[i].astype(F32)
        return total

    def sum_a(send, recv_a, rs):
        recv_a[xx] = send[xx, :, :half]
        join(recv_a.at[pick(n_x)], rs.at[0], n_x)
        return total_of(recv_a, n_x).astype(BF16)

    def sum_b(send, recv_b, rs):
        recv_b[z] = send[:, z, half:]
        join(recv_b.at[pick(n_seg)], rs.at[1], n_seg)
        return total_of(recv_b, n_seg).astype(BF16)

    spread(g_send, g_ra, g_rb, g_s, g_r, gen_scale)
    g_sa[...] = sum_a(g_send, g_ra, g_r)

    def second_a(slot, j):
        return remote(g_sa.at[j], g_ra2.at[slot], g_s.at[2], g_r.at[2], r, chip(j * n_x + xx))

    def second_b(slot, i):
        return remote(g_sb.at[i], g_rb2.at[slot], g_s.at[3], g_r.at[3], r, chip(z * n_x + i))

    for t in range(1, n_seg):
        second_a(z, z_peer(t)).start()
    g_sb[...] = sum_b(g_send, g_rb, g_r)
    for t in range(1, n_x):
        second_b(xx, x_peer(t)).start()
    g_ra2[z] = g_sa[z]
    join(g_ra2.at[pick(n_seg)], g_r.at[2], n_seg)
    total = total_of(g_ra2, n_seg)
    g_all[xx, z, :half] = total.astype(BF16)

    def gather(stage, slot, i, j):
        if stage == 0:
            ref, to = g_all.at[slot, z, low], z * n_x + i
        elif stage == 1:
            ref, to = g_all.at[xx, slot, high], j * n_x + xx
        elif stage == 2:
            ref, to = g_all.at[:, slot, low], j * n_x + xx
        else:
            ref, to = g_all.at[slot, :, high], z * n_x + i
        return remote(ref, ref, h_s.at[stage], h_r.at[stage], r, chip(to))

    for t in range(1, n_x):
        gather(0, xx, x_peer(t), z).start()
    g_rb2[xx] = g_sb[xx]
    join(g_rb2.at[pick(n_x)], g_r.at[3], n_x)
    total = total_of(g_rb2, n_x)
    g_all[xx, z, half:] = total.astype(BF16)
    for t in range(1, n_seg):
        gather(1, z, xx, z_peer(t)).start()

    join(g_all.at[pick(n_x), z, low], h_r.at[0], n_x)
    for t in range(1, n_seg):
        gather(2, z, xx, z_peer(t)).start()
    join(g_all.at[xx, pick(n_seg), high], h_r.at[1], n_seg)
    for t in range(1, n_x):
        gather(3, xx, x_peer(t), z).start()
    join(g_all.at[:, pick(n_seg), low], h_r.at[2], n_seg)

    y0 = jnp.zeros((tokens, stack), F32)
    y1 = jnp.zeros((tokens, stack), F32)
    gu = jnp.zeros((stack, stack - rank), F32)
    for t in range(n_x):
        i = x_peer(t)
        if t == 1:
            join(g_all.at[pick(n_x), :, high], h_r.at[3], n_x)
        grad = g_all[i].reshape(stack, block)
        sl = pl.ds(pl.multiple_of(i * block, 128), block)
        y0 = y0 + dot(xs[0, :, sl], grad, NT)
        y1 = y1 + dot(xs[1, :, sl], grad, NT)
        gu = gu + dot(grad, up_cat[sl, :], NN)
    gu = jnp.where(lower_mask, gu, 0.0).astype(BF16)
    in_copy(oc).wait_recv()
    mine = jnp.zeros((1, 128), F32)
    for h, y in ((0, y0), (1, y1)):
        y = (y + dot(act_cat[h], gu, NT)) * inner_cat[h].astype(F32)
        row = jnp.sum(y, axis=1, keepdims=True)
        mine = mine + jnp.sum(hot[h * tokens:(h + 1) * tokens, :] * row, axis=0, keepdims=True)
    sc0[...] = jnp.broadcast_to(mine, (8, 128))

    def p_copy(slot, n):
        return remote(sc0, sc1.at[slot], p_s, p_r, r, chip(n))

    for i in range(1, n_chip):
        p_copy(k, (k + i) % n_chip).start()

    sc1[k] = sc0[...]
    all_in(sc1.at[others], p_r)
    plane = total_of(sc1, n_chip)
    sc1s[...] = plane

    def q_copy(slot, n):
        return remote(sc1s, sc2.at[slot], q_s, q_r, n // 2, k * 2 + n % 2)

    here = r * 2 + c
    for i in range(1, 2 * n_seg):
        q_copy(here, (here + i) % (2 * n_seg)).start()

    sc2[here] = plane
    all_in(sc2.at[pl.ds(0, 2 * n_seg - 1)], q_r)
    scores = total_of(sc2, 2 * n_seg)

    entries = n_seg * rank * width
    mean_gen = jnp.sum(jnp.where(lane8 == DOMAINS - 1, scores, 0.0), axis=1, keepdims=True) / entries
    zed = scores / (math.sqrt(entries) * (mean_gen + 1e-06))
    prior_row = jnp.zeros((8, 128), F32)
    for i in range(DOMAINS - 1):
        prior_row = jnp.where(lane8 == i, prior[i], prior_row)
    train = lane8 < DOMAINS - 1
    raised = jnp.where(train, prior_row * jnp.exp(4.0 * jnp.tanh(zed / 4.0)), 0.0)
    weights = SMOOTHING / (DOMAINS - 1) + (1.0 - SMOOTHING) * raised / jnp.sum(raised, axis=1, keepdims=True)
    weights = jnp.where(train, weights, 0.0)
    set_rows(weights)

    spread(f_send, f_ra, f_rb, f_s, f_r, 1.0)
    for i in range(DOMAINS - 1):
        wout[i] = jnp.sum(jnp.where(lane == i, weights[0:1], 0.0))
    small(wout, wout_hbm, 0).start()

    def last_a(slot, s):
        return remote(f_sa.at[s], f_ra2.at[slot], f_s.at[2], f_r.at[2], s, chip(r * n_x + xx))

    def last_b(slot, i):
        return remote(f_sb.at[i], f_rb2.at[slot], f_s.at[3], f_r.at[3], z, chip(r * n_x + i))

    f_sa[...] = sum_a(f_send, f_ra, f_r)
    for t in range(1, n_seg):
        last_a(z, z_peer(t)).start()

    @pl.when(not_diag)
    def _():
        last_a(z, z).start()

    @pl.when(z == r)
    def _():
        f_ra2[z] = f_sa[z]

    f_sb[...] = sum_b(f_send, f_rb, f_r)
    for t in range(1, n_x):
        last_b(xx, x_peer(t)).start()

    @pl.when(not_diag)
    def _():
        last_b(xx, xx).start()

    @pl.when(z == r)
    def _():
        f_rb2[xx] = f_sb[xx]

    def join_last(ref, sem, count):
        @pl.when(not_diag)
        def _():
            all_in(ref, sem)

        @pl.when(z == r)
        def _():
            join(ref.at[pick(count)], sem, count)

    join_last(f_ra2, f_r.at[2], n_seg)
    rout[:half] = total_of(f_ra2, n_seg)
    small(rout.at[low], rout_hbm.at[low], 1).start()
    join_last(f_rb2, f_r.at[3], n_x)
    rout[half:] = total_of(f_rb2, n_x)
    small(rout.at[high], rout_hbm.at[high], 2).start()

    for i in range(1, n_seg):
        peer = (r + i) % n_seg

        @pl.when(e_up_from(r))
        def _():
            e_up_copy(r, peer).wait_send()

        @pl.when(e_dn_from(r))
        def _():
            e_dn_copy(r, peer).wait_send()


    for buf, sems in ((a_all, a_s), (b_all, b_s)):
        all_in(buf.at[pl.ds(0, 2)], sems.at[0])
        all_in(buf.at[0], sems.at[1])
    all_in(e_seg.at[three], ey_s)
    all_in(xs.at[c], xp_s)
    ep_copy(c).wait_send()
    all_in(act_cat.at[c], ac_s)
    all_in(inner_t.at[c], it_s)
    in_copy(c).wait_send()
    all_in(e_part.at[others], er_s)
    all_in(e_all.at[c, others], ea_s)
    all_in(sc1.at[others], p_s)
    all_in(sc2.at[pl.ds(0, 2 * n_seg - 1)], q_s)

    @pl.when(c == up_core)
    def _():
        all_in(uv.at[pl.ds(0, (n_chip - 1) * piece * (n_seg - 1))], ue_s)

    for send, sems in ((g_send, g_s), (f_send, f_s)):
        join(send.at[pick(n_x), :, low], sems.at[0], n_x)
        join(send.at[:, pick(n_seg), high], sems.at[1], n_seg)
    join(g_sa.at[pick(n_seg)], g_s.at[2], n_seg)
    join(g_sb.at[pick(n_x)], g_s.at[3], n_x)
    join(g_all.at[pick(n_x), z, low], h_s.at[0], n_x)
    join(g_all.at[xx, pick(n_seg), high], h_s.at[1], n_seg)
    join(g_all.at[:, pick(n_seg), low], h_s.at[2], n_seg)
    join(g_all.at[pick(n_x), :, high], h_s.at[3], n_x)
    join_last(f_sa, f_s.at[2], n_seg)
    join_last(f_sb, f_s.at[3], n_x)
    small(wout, wout_hbm, 0).wait()
    small(rout.at[low], rout_hbm.at[low], 1).wait()
    small(rout.at[high], rout_hbm.at[high], 2).wait()


def local(n_dp, inputs, cotangent, adapter_down, adapter_up, domain_ids, prior_weights):
    n_seg = 4
    n_chip = n_dp // 2
    n_x = n_chip // n_seg
    tokens, width = inputs.shape
    rank = adapter_down.shape[1]
    block = width // n_dp
    cols = n_x * block
    half = rank // 2
    e_rows = 3 * rank // n_chip
    down = adapter_down[0]
    up = adapter_up[0]
    piece = width // (n_seg * n_chip)
    dma = pltpu.SemaphoreType.DMA
    any_space = pl.BlockSpec(memory_space=pl.ANY)
    exchange = [
        pltpu.VMEM((n_x, n_seg, rank, block), BF16),
        pltpu.VMEM((n_x, n_seg, half, block), BF16),
        pltpu.VMEM((n_seg, n_x, half, block), BF16),
        pltpu.VMEM((n_seg, half, block), BF16),
        pltpu.VMEM((n_x, half, block), BF16),
        pltpu.VMEM((n_seg, half, block), BF16),
        pltpu.VMEM((n_x, half, block), BF16),
    ]
    scratch = [
        pltpu.SMEM(domain_ids.shape, jnp.int32),
        pltpu.SMEM(prior_weights.shape, F32),
        pltpu.SMEM((DOMAINS - 1,), F32),
        pltpu.VMEM((rank, block), F32),
        pltpu.VMEM((tokens, width), BF16),
        pltpu.VMEM((tokens, width), BF16),
        pltpu.VMEM((rank, width), BF16),
        pltpu.VMEM((width, rank), BF16),
        pltpu.VMEM((tokens, rank), F32),
        pltpu.VMEM((n_seg, piece, rank), BF16),
        pltpu.VMEM((n_seg, rank, piece), BF16),
        pltpu.VMEM((piece, 3 * rank), BF16),
        pltpu.VMEM((n_chip, e_rows, rank), F32),
        pltpu.VMEM((n_chip, e_rows, rank), F32),
        pltpu.VMEM((n_seg, e_rows, rank), F32),
        pltpu.VMEM((2, n_chip, e_rows, rank), F32),
        pltpu.VMEM((n_seg, tokens, rank), F32),
        pltpu.VMEM((n_seg, tokens, rank), F32),
        pltpu.VMEM((2, tokens, 3 * rank), BF16),
        pltpu.VMEM((2, tokens, 4 * rank), BF16),
        pltpu.VMEM((2, 4 * rank, tokens), BF16),
        pltpu.VMEM((n_x * block, 3 * rank), BF16),
        pltpu.VMEM((2, tokens, cols), BF16),
        pltpu.VMEM((2 * tokens, 128), F32),
        pltpu.VMEM((2, 8, tokens), F32),
        pltpu.VMEM((2, 4 * rank, tokens), BF16),
        pltpu.VMEM((4 * rank, 3 * rank), BF16),
        *exchange,
        pltpu.VMEM((n_x, n_seg, rank, block), BF16),
        pltpu.VMEM((8, 128), F32),
        pltpu.VMEM((n_chip, 8, 128), F32),
        pltpu.VMEM((8, 128), F32),
        pltpu.VMEM((2 * n_seg, 8, 128), F32),
        *exchange,
        dma, dma, dma, dma, dma((3,)), dma((3,)),
        dma((n_seg,)), dma((n_seg,)), dma((n_seg,)), dma((n_seg,)),
        dma, dma, dma, dma, dma, dma, dma, dma,
        dma((2,)), dma((2,)), dma((2,)), dma((2,)), dma, dma, dma, dma,
        dma, dma, dma, dma, dma, dma,
        dma((4,)), dma((4,)), dma((4,)), dma((4,)),
        dma, dma, dma, dma,
        dma((4,)), dma((4,)),
    ]
    weights, grad = pl.pallas_call(
        kernel,
        out_shape=(
            jax.ShapeDtypeStruct((DOMAINS - 1,), F32),
            jax.ShapeDtypeStruct((rank, block), F32),
        ),
        in_specs=[any_space] * 6,
        out_specs=(any_space, any_space),
        scratch_shapes=scratch,
        compiler_params=pltpu.CompilerParams(
            collective_id=0, has_side_effects=True, vmem_limit_bytes=56 * 1024 * 1024
        ),
    )(inputs, cotangent, down, up, domain_ids, prior_weights)
    return weights, grad[None]


def solution(mesh):
    return jax.shard_map(
        functools.partial(local, mesh.shape["dp"]),
        mesh=mesh,
        in_specs=(
            P("dp", None),
            P("dp", None),
            P("segment", None, None),
            P("segment", None, None),
            P(),
            P(),
        ),
        out_specs=(P(), P("segment", None, "dp")),
        check_vma=False,
    )
```

```python
import functools
import math

import jax
import jax.numpy as jnp
from jax import lax
from jax.experimental import pallas as pl
from jax.experimental.pallas import tpu as pltpu
from jax.sharding import PartitionSpec as P

DOMAINS = 9
TOK_MICRO = 56
SMOOTHING = 0.5
MESH = pl.DeviceIdType.MESH
F32 = jnp.float32
BF16 = jnp.bfloat16
NT = (((1,), (1,)), ((), ()))
NN = (((1,), (0,)), ((), ()))
TN = (((0,), (0,)), ((), ()))


def dot(a, b, dims):
    return lax.dot_general(a, b, dims, preferred_element_type=F32)


def remote(src, dst, send, recv, seg, dp):
    return pltpu.make_async_remote_copy(
        src_ref=src, dst_ref=dst, send_sem=send, recv_sem=recv, device_id=(seg, dp), device_id_type=MESH
    )


def all_in(ref, sem):
    pltpu.make_async_copy(ref, ref, sem).wait()


def each(lo, hi, body):
    def step(i, carry):
        body(i)
        return carry

    lax.fori_loop(lo, hi, step, 0)


def kernel(
    x_hbm, cot_hbm, down_hbm, up_hbm, ids_hbm, prior_hbm,
    wout_hbm, rout_hbm,
    ids, prior, wout, rout,
    xv, cv, dv, uv, acc, e_up, e_dn, e_cat, e_part, e_rs, e_seg, e_all, a_all, b_all, act_cat, inner_cat, inner_t,
    up_cat, xs, hot, row_w, lhs_t, cross,
    g_send, g_ra, g_rb, g_sa, g_sb, g_ra2, g_rb2, g_all, sc0, sc1, sc1s, sc2,
    f_send, f_ra, f_rb, f_sa, f_sb, f_ra2, f_rb2,
    s_x, s_c, s_d, s_u, s_loc, s_small,
    eu_s, eu_r, ed_s, ed_r, er_s, er_r, ey_s, ey_r, ea_s, ea_r, ep_s, ep_r,
    a_s, a_r, b_s, b_r, ue_s, ue_r, xp_s, xp_r, ac_s, ac_r, in_s, in_r, it_s, it_r,
    g_s, g_r, h_s, h_r, p_s, p_r, q_s, q_r, f_s, f_r,
):
    n_seg = 4
    n_chip = e_part.shape[0]
    n_x = n_chip // n_seg
    tokens, width = x_hbm.shape
    rank = down_hbm.shape[0]
    block = width // (2 * n_chip)
    cols = n_x * block
    chunks = 8
    kc = width // chunks
    half = rank // 2
    low, high = pl.ds(0, half), pl.ds(half, half)
    piece = width // (n_seg * n_chip)
    per = block // piece

    r = lax.axis_index("segment")
    dp = lax.axis_index("dp")
    c = dp % 2
    k = dp // 2
    z = k // n_x
    xx = k % n_x
    oc = 1 - c
    partner = k * 2 + oc
    up_core = (k // per) % 2

    def chip(n):
        return n * 2 + c

    def x_peer(i):
        return (xx + i) % n_x

    def z_peer(i):
        return (z + i) % n_seg

    bar = pltpu.get_barrier_semaphore()

    def greet(seg, d):
        pl.semaphore_signal(bar, inc=1, device_id=(seg, d), device_id_type=MESH)

    def greet_plane(i):
        greet(r, chip((k + i) % n_chip))

    each(1, n_chip, greet_plane)

    def greet_seg(i):
        greet((r + i) % n_seg, dp)
        greet((r + i) % n_seg, partner)

    each(1, n_seg, greet_seg)
    greet(r, partner)

    not_diag = z != r
    for i in range(n_seg):
        j = (z + i) % n_seg
        if i == 0:
            @pl.when(not_diag)
            def _():
                greet(z, chip(r * n_x + xx))
                greet(z, chip(r * n_x + xx))
        else:
            greet(j, chip(r * n_x + xx))
        j = (r + i) % n_seg
        if i == 0:
            @pl.when(not_diag)
            def _():
                greet(z, chip(r * n_x + xx))
                greet(z, chip(r * n_x + xx))
        else:
            greet(z, chip(j * n_x + xx))
    for i in range(1, n_x):
        j = (xx + i) % n_x
        greet(z, chip(r * n_x + j))
        greet(z, chip(r * n_x + j))

    def piece_of(seg):
        return pl.ds(pl.multiple_of((seg * n_chip + k) * piece, 128), piece)

    def own_dn():
        return pltpu.make_async_copy(down_hbm.at[:, piece_of(r)], e_dn.at[r], s_loc.at[0])

    def own_up():
        return pltpu.make_async_copy(up_hbm.at[piece_of(r), :], e_up.at[r], s_loc.at[1])

    def small(src, dst, i):
        return pltpu.make_async_copy(src, dst, s_small.at[i])

    small(ids_hbm, ids, 0).start()
    small(prior_hbm, prior, 1).start()
    own_dn().start()
    own_up().start()
    pltpu.make_async_copy(down_hbm, dv, s_d).start()

    x_copy = pltpu.make_async_copy(x_hbm, xv, s_x)
    c_copy = pltpu.make_async_copy(cot_hbm, cv, s_c)
    x_copy.start()
    pltpu.make_async_copy(up_hbm, uv, s_u).start()
    c_copy.start()

    def own_cols(i, core):
        return pl.ds(((r * n_x + i) * 2 + core) * block, block)

    def xe_copy(i):
        return pltpu.make_async_copy(
            x_hbm.at[:, own_cols(i, c)], xs.at[c, :, pl.ds(i * block, block)], s_loc.at[2]
        )

    each(0, n_x, lambda i: xe_copy(i).start())

    lane = lax.broadcasted_iota(jnp.int32, (1, 128), 1)

    def count(i, total):
        return total + jnp.where(lane == ids[i], 1.0, 0.0)

    small(ids_hbm, ids, 0).wait()
    small(prior_hbm, prior, 1).wait()
    counts = lax.fori_loop(0, ids.shape[0], count, jnp.zeros((1, 128), F32))
    scale = 1.0 / (counts * TOK_MICRO)
    micros = 2 * tokens // TOK_MICRO

    def fill(m):
        name = ids[k * micros + m]
        row = jnp.where(lane == name, scale, 0.0)
        hot[pl.ds(pl.multiple_of(m * TOK_MICRO, 8), TOK_MICRO), :] = jnp.broadcast_to(row, (TOK_MICRO, 128))

    each(0, micros, fill)

    def set_rows(weights):
        for h in range(2):
            row_w[h] = lax.dot_general(
                weights,
                hot[h * tokens:(h + 1) * tokens, :],
                NT,
                precision=lax.Precision.HIGHEST,
                preferred_element_type=F32,
            )

    lane8 = lax.broadcasted_iota(jnp.int32, (8, 128), 1)
    gen_scale = jnp.sum(jnp.where(lane == DOMAINS - 1, scale, 0.0), axis=1, keepdims=True)
    set_rows(jnp.where(lane8 == DOMAINS - 1, 1.0, 0.0))
    for h in range(2):
        row_w[h] = jnp.where(row_w[h] > 0.0, 1.0, 0.0)

    pl.semaphore_wait(bar, (n_chip - 1) + 2 * (n_seg - 1) + 1 + 2 * (n_seg + n_x) - jnp.where(not_diag, 0, 4))

    def e_up_from(j):
        return (j < n_seg - 1) & ((c == 0) & (j == 0) | (c == 1) & (j >= 1) | (c == up_core))

    def e_dn_from(j):
        return j >= 1 + c

    def e_up_copy(slot, peer):
        return remote(up_hbm.at[piece_of(peer), :], e_up.at[slot], eu_s.at[peer], eu_r.at[slot], peer, dp)

    def e_dn_copy(slot, peer):
        return remote(down_hbm.at[:, piece_of(peer)], e_dn.at[slot], ed_s.at[peer], ed_r.at[slot], peer, dp)

    for i in range(1, n_seg):
        peer = (r + i) % n_seg

        @pl.when(e_up_from(r))
        def _():
            e_up_copy(r, peer).start()

        @pl.when(e_dn_from(r))
        def _():
            e_dn_copy(r, peer).start()

    def xp_copy(i, slot_core, col_core):
        return remote(
            x_hbm.at[:, own_cols(i, col_core)],
            xs.at[slot_core, :, pl.ds(i * block, block)],
            xp_s,
            xp_r,
            r,
            partner,
        )

    each(0, n_x, lambda i: xp_copy(i, c, oc).start())

    pltpu.make_async_copy(down_hbm, dv, s_d).wait()
    acc[...] = jnp.zeros_like(acc)
    x_copy.wait()

    def a_step(i):
        sl = pl.ds(pl.multiple_of(i * kc, 128), kc)
        acc[...] += dot(xv[:, sl], dv[:, sl], NT)

    each(0, chunks, a_step)
    a_all[r] = acc[...]

    def seg_copy(buf, send, recv, slot, peer):
        return remote(buf.at[slot], buf.at[slot], send, recv, peer, dp)


    behind, ahead = (r + n_seg - 1) % n_seg, (r + 1) % n_seg
    first_rows, last_rows = pl.ds(0, tokens // 2), pl.ds(tokens // 2, tokens // 2)

    def near(buf, send, recv):
        remote(buf.at[r], buf.at[r], send.at[0], recv.at[0], ahead, dp).start()
        remote(buf.at[r], buf.at[r], send.at[0], recv.at[0], behind, dp).start()

    def pass_on(buf, send, recv):
        all_in(buf.at[pl.ds(0, 2)], recv.at[0])
        up_ref = buf.at[behind, first_rows]
        down_ref = buf.at[ahead, last_rows]
        remote(up_ref, up_ref, send.at[1], recv.at[1], ahead, dp).start()
        remote(down_ref, down_ref, send.at[1], recv.at[1], behind, dp).start()

    near(a_all, a_s, a_r)

    three = pl.ds(0, n_seg - 1)
    others = pl.ds(0, n_chip - 1)

    for j in range(n_seg):
        @pl.when((j != r) & e_up_from(j))
        def _():
            e_up_copy(j, (r + 1) % n_seg).wait_recv()

        @pl.when((j != r) & e_dn_from(j))
        def _():
            e_dn_copy(j, (r + 1) % n_seg).wait_recv()

    own_dn().wait()
    own_up().wait()
    e_rows = e_part.shape[1]
    e_mats = []
    for m, (da, ua) in enumerate(((2, 1), (3, 1), (3, 2))):
        e_mats.append(dot(e_dn[(1 - c) * (m + 1) + c * da], e_up[c * ua], NN))
    e_part[...] = jnp.concatenate(e_mats, axis=0).reshape(n_chip, e_rows, rank)

    def er_copy(slot, n):
        return remote(e_part.at[n], e_rs.at[slot], er_s, er_r, r, chip(n))

    each(1, n_chip, lambda i: er_copy(k, (k + i) % n_chip).start())

    def up_slot(n):
        return up_cat.at[pl.ds(pl.multiple_of((n // (2 * per)) * block + (n % per) * piece, 128), piece)]

    def ue_copy(slot, n):
        return remote(e_cat, up_slot(slot), ue_s, ue_r, r, chip(n))

    @pl.when(c == up_core)
    def _():
        for j in range(n_seg - 1):
            e_cat[:, j * rank:(j + 1) * rank] = e_up[j]
        each(1, n_chip, lambda i: ue_copy(k, (k + i) % n_chip).start())
        up_slot(k)[...] = e_cat[...]

    pltpu.make_async_copy(up_hbm, uv, s_u).wait()
    acc[...] = jnp.zeros_like(acc)
    c_copy.wait()

    def b_step(i):
        sl = pl.ds(pl.multiple_of(i * kc, 128), kc)
        acc[...] += dot(cv[:, sl], uv[sl, :], NN)

    each(0, chunks, b_step)
    b_all[r] = acc[...]

    e_rs[k] = e_part[k]
    all_in(e_rs.at[others], er_r)
    total = e_rs[0]
    for n in range(1, n_chip):
        total = total + e_rs[n]
    e_seg[r] = total
    for i in range(1, n_seg):
        seg_copy(e_seg, ey_s, ey_r, r, (r + i) % n_seg).start()
    near(b_all, b_s, b_r)
    all_in(e_seg.at[three], ey_r)
    e_all[c, k] = e_seg[0] + e_seg[1] + e_seg[2] + e_seg[3]

    def ea_copy(slot, n):
        return remote(e_all.at[c, slot], e_all.at[c, slot], ea_s, ea_r, r, chip(n))

    each(1, n_chip, lambda i: ea_copy(k, (k + i) % n_chip).start())

    pass_on(a_all, a_s, a_r)

    all_in(e_all.at[c, others], ea_r)

    def ep_copy(core):
        return remote(e_all.at[core], e_all.at[core], ep_s, ep_r, r, partner)

    ep_copy(c).start()
    pass_on(b_all, b_s, b_r)
    ep_copy(oc).wait_recv()

    all_in(a_all.at[0], a_r.at[1])

    def two_terms(m):
        high_part = m.astype(BF16)
        return high_part, (m - high_part.astype(F32)).astype(BF16)

    lower = {}
    for core, pairs in ((0, ((1, 0), (2, 0), (3, 0))), (1, ((2, 1), (3, 1), (3, 2)))):
        mats = e_all[core].reshape(3 * rank, rank)
        for m, pair in enumerate(pairs):
            lower[pair] = two_terms(mats[m * rank:(m + 1) * rank])

    def act_copy(j, core):
        ref = act_cat.at[core, :, pl.ds(j * rank, rank)]
        return remote(ref, ref, ac_s, ac_r, r, partner)

    def in_copy(core):
        return remote(inner_cat.at[core], inner_cat.at[core], in_s, in_r, r, partner)

    def it_copy(j, core):
        ref = inner_t.at[core, pl.ds(j * rank, rank)]
        return remote(ref, ref, it_s, it_r, r, partner)

    slopes = []
    acts = []
    for s in range(n_seg):
        pre = a_all[s]
        for j in range(s):
            pre = pre + dot(acts[j], lower[(s, j)][0], NT) + dot(acts[j], lower[(s, j)][1], NT)
        sig = 1.0 / (1.0 + jnp.exp(-pre))
        slopes.append(sig * (1.0 + pre * (1.0 - sig)))
        if s < n_seg - 1:
            act = (pre * sig).astype(BF16)
            acts.append(act)
            act_cat[c, :, s * rank:(s + 1) * rank] = act
            act_copy(s, c).start()

    all_in(b_all.at[0], b_r.at[1])

    inners = [None] * n_seg
    for s in reversed(range(n_seg)):
        pulled = b_all[s]
        for j in range(s + 1, n_seg):
            pulled = pulled + dot(inners[j], lower[(j, s)][0], NN) + dot(inners[j], lower[(j, s)][1], NN)
        wide = pulled * slopes[s]
        inner = wide.astype(BF16)
        inners[s] = inner
        inner_t[c, s * rank:(s + 1) * rank, :] = wide.T.astype(BF16)
        it_copy(s, c).start()
        inner_cat[c, :, s * rank:(s + 1) * rank] = inner

    in_copy(c).start()

    all_in(xs.at[c], s_loc.at[2])
    all_in(xs.at[oc], xp_r)

    @pl.when(c == up_core)
    def _():
        all_in(up_cat.at[pl.ds(0, n_x * block - piece)], ue_r)

    @pl.when(c != up_core)
    def _():
        all_in(up_cat, ue_r)

    all_in(act_cat.at[oc], ac_r)
    all_in(inner_t.at[oc], it_r)
    stack = n_seg * rank
    lower_mask = (
        lax.broadcasted_iota(jnp.int32, (stack, stack - rank), 0) // rank
        > lax.broadcasted_iota(jnp.int32, (stack, stack - rank), 1) // rank
    )

    def set_weighted():
        for h in range(2):
            weight = row_w[h, 0:1, :]
            for s in range(n_seg):
                rows = slice(s * rank, (s + 1) * rank)
                lhs_t[h, rows, :] = (inner_t[h, rows, :].astype(F32) * weight).astype(BF16)
        both = dot(lhs_t[0], act_cat[0], NN) + dot(lhs_t[1], act_cat[1], NN)
        cross[...] = jnp.where(lower_mask, both, 0.0).astype(BF16)

    def weighted_grad(i):
        sl = pl.ds(pl.multiple_of(i * block, 128), block)
        total = dot(lhs_t[0], xs[0, :, sl], NN) + dot(lhs_t[1], xs[1, :, sl], NN)
        return total + dot(cross[...], up_cat[pl.ds(pl.multiple_of(i * block, 128), block), :], NT)

    def first_a(send, recv, ss, rs, slot, i):
        return remote(send.at[i, :, low], recv.at[slot], ss.at[0], rs.at[0], r, chip(z * n_x + i))

    def first_b(send, recv, ss, rs, slot, j):
        return remote(send.at[:, j, high], recv.at[slot], ss.at[1], rs.at[1], r, chip(j * n_x + xx))

    def spread(send, recv_a, recv_b, ss, rs, factor):
        set_weighted()

        def column_block(t):
            i = (xx + 1 + t) % n_x
            send[i] = (weighted_grad(i) * factor).reshape(n_seg, rank, block).astype(BF16)

            @pl.when(i != xx)
            def _():
                first_a(send, recv_a, ss, rs, xx, i).start()

        each(0, n_x, column_block)
        for t in range(1, n_seg):
            first_b(send, recv_b, ss, rs, z, z_peer(t)).start()

    def pick(count):
        return pl.ds(0, count - 1)

    def join(ref, sem, axis_len):
        if axis_len > 1:
            all_in(ref, sem)

    def total_of(ref, count):
        total = ref[0].astype(F32)
        for i in range(1, count):
            total = total + ref[i].astype(F32)
        return total

    def sum_a(send, recv_a, rs):
        recv_a[xx] = send[xx, :, :half]
        join(recv_a.at[pick(n_x)], rs.at[0], n_x)
        return total_of(recv_a, n_x).astype(BF16)

    def sum_b(send, recv_b, rs):
        recv_b[z] = send[:, z, half:]
        join(recv_b.at[pick(n_seg)], rs.at[1], n_seg)
        return total_of(recv_b, n_seg).astype(BF16)

    spread(g_send, g_ra, g_rb, g_s, g_r, gen_scale)
    g_sa[...] = sum_a(g_send, g_ra, g_r)

    def second_a(slot, j):
        return remote(g_sa.at[j], g_ra2.at[slot], g_s.at[2], g_r.at[2], r, chip(j * n_x + xx))

    def second_b(slot, i):
        return remote(g_sb.at[i], g_rb2.at[slot], g_s.at[3], g_r.at[3], r, chip(z * n_x + i))

    for t in range(1, n_seg):
        second_a(z, z_peer(t)).start()
    g_sb[...] = sum_b(g_send, g_rb, g_r)
    for t in range(1, n_x):
        second_b(xx, x_peer(t)).start()
    g_ra2[z] = g_sa[z]
    join(g_ra2.at[pick(n_seg)], g_r.at[2], n_seg)
    total = total_of(g_ra2, n_seg)
    g_all[xx, z, :half] = total.astype(BF16)

    def gather(stage, slot, i, j):
        if stage == 0:
            ref, to = g_all.at[slot, z, low], z * n_x + i
        elif stage == 1:
            ref, to = g_all.at[xx, slot, high], j * n_x + xx
        elif stage == 2:
            ref, to = g_all.at[:, slot, low], j * n_x + xx
        else:
            ref, to = g_all.at[slot, :, high], z * n_x + i
        return remote(ref, ref, h_s.at[stage], h_r.at[stage], r, chip(to))

    for t in range(1, n_x):
        gather(0, xx, x_peer(t), z).start()
    g_rb2[xx] = g_sb[xx]
    join(g_rb2.at[pick(n_x)], g_r.at[3], n_x)
    total = total_of(g_rb2, n_x)
    g_all[xx, z, half:] = total.astype(BF16)
    for t in range(1, n_seg):
        gather(1, z, xx, z_peer(t)).start()

    join(g_all.at[pick(n_x), z, low], h_r.at[0], n_x)
    for t in range(1, n_seg):
        gather(2, z, xx, z_peer(t)).start()
    join(g_all.at[xx, pick(n_seg), high], h_r.at[1], n_seg)
    for t in range(1, n_x):
        gather(3, xx, x_peer(t), z).start()
    join(g_all.at[:, pick(n_seg), low], h_r.at[2], n_seg)

    y0 = jnp.zeros((tokens, stack), F32)
    y1 = jnp.zeros((tokens, stack), F32)
    gu = jnp.zeros((stack, stack - rank), F32)
    for t in range(n_x):
        i = x_peer(t)
        if t == 1:
            join(g_all.at[pick(n_x), :, high], h_r.at[3], n_x)
        grad = g_all[i].reshape(stack, block)
        sl = pl.ds(pl.multiple_of(i * block, 128), block)
        y0 = y0 + dot(xs[0, :, sl], grad, NT)
        y1 = y1 + dot(xs[1, :, sl], grad, NT)
        gu = gu + dot(grad, up_cat[sl, :], NN)
    gu = jnp.where(lower_mask, gu, 0.0).astype(BF16)
    in_copy(oc).wait_recv()
    mine = jnp.zeros((1, 128), F32)
    for h, y in ((0, y0), (1, y1)):
        y = (y + dot(act_cat[h], gu, NT)) * inner_cat[h].astype(F32)
        row = jnp.sum(y, axis=1, keepdims=True)
        mine = mine + jnp.sum(hot[h * tokens:(h + 1) * tokens, :] * row, axis=0, keepdims=True)
    sc0[...] = jnp.broadcast_to(mine, (8, 128))

    def p_copy(slot, n):
        return remote(sc0, sc1.at[slot], p_s, p_r, r, chip(n))

    for i in range(1, n_chip):
        p_copy(k, (k + i) % n_chip).start()

    sc1[k] = sc0[...]
    all_in(sc1.at[others], p_r)
    plane = total_of(sc1, n_chip)
    sc1s[...] = plane

    def q_copy(slot, n):
        return remote(sc1s, sc2.at[slot], q_s, q_r, n // 2, k * 2 + n % 2)

    here = r * 2 + c
    for i in range(1, 2 * n_seg):
        q_copy(here, (here + i) % (2 * n_seg)).start()

    sc2[here] = plane
    all_in(sc2.at[pl.ds(0, 2 * n_seg - 1)], q_r)
    scores = total_of(sc2, 2 * n_seg)

    entries = n_seg * rank * width
    mean_gen = jnp.sum(jnp.where(lane8 == DOMAINS - 1, scores, 0.0), axis=1, keepdims=True) / entries
    zed = scores / (math.sqrt(entries) * (mean_gen + 1e-06))
    prior_row = jnp.zeros((8, 128), F32)
    for i in range(DOMAINS - 1):
        prior_row = jnp.where(lane8 == i, prior[i], prior_row)
    train = lane8 < DOMAINS - 1
    raised = jnp.where(train, prior_row * jnp.exp(4.0 * jnp.tanh(zed / 4.0)), 0.0)
    weights = SMOOTHING / (DOMAINS - 1) + (1.0 - SMOOTHING) * raised / jnp.sum(raised, axis=1, keepdims=True)
    weights = jnp.where(train, weights, 0.0)
    set_rows(weights)

    spread(f_send, f_ra, f_rb, f_s, f_r, 1.0)
    for i in range(DOMAINS - 1):
        wout[i] = jnp.sum(jnp.where(lane == i, weights[0:1], 0.0))
    small(wout, wout_hbm, 0).start()

    def last_a(slot, s):
        return remote(f_sa.at[s], f_ra2.at[slot], f_s.at[2], f_r.at[2], s, chip(r * n_x + xx))

    def last_b(slot, i):
        return remote(f_sb.at[i], f_rb2.at[slot], f_s.at[3], f_r.at[3], z, chip(r * n_x + i))

    f_sa[...] = sum_a(f_send, f_ra, f_r)
    for t in range(1, n_seg):
        last_a(z, z_peer(t)).start()

    @pl.when(not_diag)
    def _():
        last_a(z, z).start()

    @pl.when(z == r)
    def _():
        f_ra2[z] = f_sa[z]

    f_sb[...] = sum_b(f_send, f_rb, f_r)
    for t in range(1, n_x):
        last_b(xx, x_peer(t)).start()

    @pl.when(not_diag)
    def _():
        last_b(xx, xx).start()

    @pl.when(z == r)
    def _():
        f_rb2[xx] = f_sb[xx]

    def join_last(ref, sem, count):
        @pl.when(not_diag)
        def _():
            all_in(ref, sem)

        @pl.when(z == r)
        def _():
            join(ref.at[pick(count)], sem, count)

    join_last(f_ra2, f_r.at[2], n_seg)
    rout[:half] = total_of(f_ra2, n_seg)
    small(rout.at[low], rout_hbm.at[low], 1).start()
    join_last(f_rb2, f_r.at[3], n_x)
    rout[half:] = total_of(f_rb2, n_x)
    small(rout.at[high], rout_hbm.at[high], 2).start()

    for i in range(1, n_seg):
        peer = (r + i) % n_seg

        @pl.when(e_up_from(r))
        def _():
            e_up_copy(r, peer).wait_send()

        @pl.when(e_dn_from(r))
        def _():
            e_dn_copy(r, peer).wait_send()


    for buf, sems in ((a_all, a_s), (b_all, b_s)):
        all_in(buf.at[pl.ds(0, 2)], sems.at[0])
        all_in(buf.at[0], sems.at[1])
    all_in(e_seg.at[three], ey_s)
    all_in(xs.at[c], xp_s)
    ep_copy(c).wait_send()
    all_in(act_cat.at[c], ac_s)
    all_in(inner_t.at[c], it_s)
    in_copy(c).wait_send()
    all_in(e_part.at[others], er_s)
    all_in(e_all.at[c, others], ea_s)
    all_in(sc1.at[others], p_s)
    all_in(sc2.at[pl.ds(0, 2 * n_seg - 1)], q_s)

    @pl.when(c == up_core)
    def _():
        all_in(uv.at[pl.ds(0, (n_chip - 1) * piece * (n_seg - 1))], ue_s)

    for send, sems in ((g_send, g_s), (f_send, f_s)):
        join(send.at[pick(n_x), :, low], sems.at[0], n_x)
        join(send.at[:, pick(n_seg), high], sems.at[1], n_seg)
    join(g_sa.at[pick(n_seg)], g_s.at[2], n_seg)
    join(g_sb.at[pick(n_x)], g_s.at[3], n_x)
    join(g_all.at[pick(n_x), z, low], h_s.at[0], n_x)
    join(g_all.at[xx, pick(n_seg), high], h_s.at[1], n_seg)
    join(g_all.at[:, pick(n_seg), low], h_s.at[2], n_seg)
    join(g_all.at[pick(n_x), :, high], h_s.at[3], n_x)
    join_last(f_sa, f_s.at[2], n_seg)
    join_last(f_sb, f_s.at[3], n_x)
    small(wout, wout_hbm, 0).wait()
    small(rout.at[low], rout_hbm.at[low], 1).wait()
    small(rout.at[high], rout_hbm.at[high], 2).wait()


def hand_over(weights, grad, wout, rout):
    for i in range(DOMAINS - 1):
        wout[i] = weights[i]
    rout[0] = grad[...]


def local(n_dp, inputs, cotangent, adapter_down, adapter_up, domain_ids, prior_weights):
    n_seg = 4
    n_chip = n_dp // 2
    n_x = n_chip // n_seg
    tokens, width = inputs.shape
    rank = adapter_down.shape[1]
    block = width // n_dp
    cols = n_x * block
    half = rank // 2
    e_rows = 3 * rank // n_chip
    down = adapter_down[0]
    up = adapter_up[0]
    piece = width // (n_seg * n_chip)
    dma = pltpu.SemaphoreType.DMA
    any_space = pl.BlockSpec(memory_space=pl.ANY)
    exchange = [
        pltpu.VMEM((n_x, n_seg, rank, block), BF16),
        pltpu.VMEM((n_x, n_seg, half, block), BF16),
        pltpu.VMEM((n_seg, n_x, half, block), BF16),
        pltpu.VMEM((n_seg, half, block), BF16),
        pltpu.VMEM((n_x, half, block), BF16),
        pltpu.VMEM((n_seg, half, block), BF16),
        pltpu.VMEM((n_x, half, block), BF16),
    ]
    scratch = [
        pltpu.SMEM(domain_ids.shape, jnp.int32),
        pltpu.SMEM(prior_weights.shape, F32),
        pltpu.SMEM((DOMAINS - 1,), F32),
        pltpu.VMEM((rank, block), F32),
        pltpu.VMEM((tokens, width), BF16),
        pltpu.VMEM((tokens, width), BF16),
        pltpu.VMEM((rank, width), BF16),
        pltpu.VMEM((width, rank), BF16),
        pltpu.VMEM((tokens, rank), F32),
        pltpu.VMEM((n_seg, piece, rank), BF16),
        pltpu.VMEM((n_seg, rank, piece), BF16),
        pltpu.VMEM((piece, 3 * rank), BF16),
        pltpu.VMEM((n_chip, e_rows, rank), F32),
        pltpu.VMEM((n_chip, e_rows, rank), F32),
        pltpu.VMEM((n_seg, e_rows, rank), F32),
        pltpu.VMEM((2, n_chip, e_rows, rank), F32),
        pltpu.VMEM((n_seg, tokens, rank), F32),
        pltpu.VMEM((n_seg, tokens, rank), F32),
        pltpu.VMEM((2, tokens, 3 * rank), BF16),
        pltpu.VMEM((2, tokens, 4 * rank), BF16),
        pltpu.VMEM((2, 4 * rank, tokens), BF16),
        pltpu.VMEM((n_x * block, 3 * rank), BF16),
        pltpu.VMEM((2, tokens, cols), BF16),
        pltpu.VMEM((2 * tokens, 128), F32),
        pltpu.VMEM((2, 8, tokens), F32),
        pltpu.VMEM((2, 4 * rank, tokens), BF16),
        pltpu.VMEM((4 * rank, 3 * rank), BF16),
        *exchange,
        pltpu.VMEM((n_x, n_seg, rank, block), BF16),
        pltpu.VMEM((8, 128), F32),
        pltpu.VMEM((n_chip, 8, 128), F32),
        pltpu.VMEM((8, 128), F32),
        pltpu.VMEM((2 * n_seg, 8, 128), F32),
        *exchange,
        dma, dma, dma, dma, dma((3,)), dma((3,)),
        dma((n_seg,)), dma((n_seg,)), dma((n_seg,)), dma((n_seg,)),
        dma, dma, dma, dma, dma, dma, dma, dma,
        dma((2,)), dma((2,)), dma((2,)), dma((2,)), dma, dma, dma, dma,
        dma, dma, dma, dma, dma, dma,
        dma((4,)), dma((4,)), dma((4,)), dma((4,)),
        dma, dma, dma, dma,
        dma((4,)), dma((4,)),
    ]
    weights, grad = pl.pallas_call(
        kernel,
        out_shape=(
            jax.ShapeDtypeStruct((DOMAINS - 1,), F32),
            jax.ShapeDtypeStruct((rank, block), F32),
        ),
        in_specs=[any_space] * 6,
        out_specs=(any_space, any_space),
        scratch_shapes=scratch,
        compiler_params=pltpu.CompilerParams(
            collective_id=0, has_side_effects=True, vmem_limit_bytes=56 * 1024 * 1024
        ),
    )(inputs, cotangent, down, up, domain_ids, prior_weights)
    return pl.pallas_call(
        hand_over,
        out_shape=(
            jax.ShapeDtypeStruct((DOMAINS - 1,), F32),
            jax.ShapeDtypeStruct((1, rank, block), F32),
        ),
        in_specs=[pl.BlockSpec(memory_space=pltpu.SMEM), pl.BlockSpec(memory_space=pltpu.VMEM)],
        out_specs=(pl.BlockSpec(memory_space=pltpu.SMEM), pl.BlockSpec(memory_space=pltpu.VMEM)),
    )(weights, grad)


def solution(mesh):
    return jax.shard_map(
        functools.partial(local, mesh.shape["dp"]),
        mesh=mesh,
        in_specs=(
            P("dp", None),
            P("dp", None),
            P("segment", None, None),
            P("segment", None, None),
            P(),
            P(),
        ),
        out_specs=(P(), P("segment", None, "dp")),
        check_vma=False,
    )
```

```python
import functools
import math

import jax
import jax.numpy as jnp
from jax import lax
from jax.experimental import pallas as pl
from jax.experimental.pallas import tpu as pltpu
from jax.sharding import PartitionSpec as P

DOMAINS = 9
TOK_MICRO = 56
SMOOTHING = 0.5
MESH = pl.DeviceIdType.MESH
F32 = jnp.float32
BF16 = jnp.bfloat16
NT = (((1,), (1,)), ((), ()))
NN = (((1,), (0,)), ((), ()))
TN = (((0,), (0,)), ((), ()))


def dot(a, b, dims):
    return lax.dot_general(a, b, dims, preferred_element_type=F32)


def remote(src, dst, send, recv, seg, dp):
    return pltpu.make_async_remote_copy(
        src_ref=src, dst_ref=dst, send_sem=send, recv_sem=recv, device_id=(seg, dp), device_id_type=MESH
    )


def all_in(ref, sem):
    pltpu.make_async_copy(ref, ref, sem).wait()


def each(lo, hi, body):
    def step(i, carry):
        body(i)
        return carry

    lax.fori_loop(lo, hi, step, 0)


def kernel(
    x_hbm, cot_hbm, down_hbm, up_hbm, ids_hbm, prior_hbm,
    wout_hbm, rout_hbm,
    ids, prior, wout, rout,
    xv, cv, dv, uv, acc, e_up, e_dn, e_cat, e_part, e_rs, e_seg, e_all, a_all, b_all, act_cat, inner_cat, inner_t,
    up_cat, xs, hot, row_w, lhs_t, cross,
    g_send, g_ra, g_rb, g_sa, g_sb, g_ra2, g_rb2, g_all, sc0, sc1, sc1s, sc2,
    f_send, f_ra, f_rb, f_sa, f_sb, f_ra2, f_rb2,
    s_x, s_c, s_d, s_u, s_loc, s_small,
    eu_s, eu_r, ed_s, ed_r, er_s, er_r, ey_s, ey_r, ea_s, ea_r, ep_s, ep_r,
    a_s, a_r, b_s, b_r, ue_s, ue_r, xp_s, xp_r, ac_s, ac_r, in_s, in_r, it_s, it_r,
    g_s, g_r, h_s, h_r, p_s, p_r, q_s, q_r, f_s, f_r,
):
    n_seg = 4
    n_chip = e_part.shape[0]
    n_x = n_chip // n_seg
    tokens, width = x_hbm.shape
    rank = down_hbm.shape[0]
    block = width // (2 * n_chip)
    cols = n_x * block
    chunks = 8
    kc = width // chunks
    half = rank // 2
    low, high = pl.ds(0, half), pl.ds(half, half)
    piece = width // (n_seg * n_chip)
    per = block // piece

    r = lax.axis_index("segment")
    dp = lax.axis_index("dp")
    c = dp % 2
    k = dp // 2
    z = k // n_x
    xx = k % n_x
    oc = 1 - c
    partner = k * 2 + oc
    up_core = (k // per) % 2

    def chip(n):
        return n * 2 + c

    def x_peer(i):
        return (xx + i) % n_x

    def z_peer(i):
        return (z + i) % n_seg

    bar = pltpu.get_barrier_semaphore()

    def greet(seg, d):
        pl.semaphore_signal(bar, inc=1, device_id=(seg, d), device_id_type=MESH)

    def greet_plane(i):
        greet(r, chip((k + i) % n_chip))

    each(1, n_chip, greet_plane)

    def greet_seg(i):
        greet((r + i) % n_seg, dp)
        greet((r + i) % n_seg, partner)

    each(1, n_seg, greet_seg)
    greet(r, partner)

    not_diag = z != r
    for i in range(n_seg):
        j = (z + i) % n_seg
        if i == 0:
            @pl.when(not_diag)
            def _():
                greet(z, chip(r * n_x + xx))
                greet(z, chip(r * n_x + xx))
        else:
            greet(j, chip(r * n_x + xx))
        j = (r + i) % n_seg
        if i == 0:
            @pl.when(not_diag)
            def _():
                greet(z, chip(r * n_x + xx))
                greet(z, chip(r * n_x + xx))
        else:
            greet(z, chip(j * n_x + xx))
    for i in range(1, n_x):
        j = (xx + i) % n_x
        greet(z, chip(r * n_x + j))
        greet(z, chip(r * n_x + j))

    def piece_of(seg):
        return pl.ds(pl.multiple_of((seg * n_chip + k) * piece, 128), piece)

    def own_dn():
        return pltpu.make_async_copy(down_hbm.at[:, piece_of(r)], e_dn.at[r], s_loc.at[0])

    def own_up():
        return pltpu.make_async_copy(up_hbm.at[piece_of(r), :], e_up.at[r], s_loc.at[1])

    def small(src, dst, i):
        return pltpu.make_async_copy(src, dst, s_small.at[i])

    small(ids_hbm, ids, 0).start()
    small(prior_hbm, prior, 1).start()
    own_dn().start()
    own_up().start()
    pltpu.make_async_copy(down_hbm, dv, s_d).start()

    x_copy = pltpu.make_async_copy(x_hbm, xv, s_x)
    c_copy = pltpu.make_async_copy(cot_hbm, cv, s_c)
    x_copy.start()
    pltpu.make_async_copy(up_hbm, uv, s_u).start()
    c_copy.start()

    def own_cols(i, core):
        return pl.ds(((r * n_x + i) * 2 + core) * block, block)

    def xe_copy(i):
        return pltpu.make_async_copy(
            x_hbm.at[:, own_cols(i, c)], xs.at[c, :, pl.ds(i * block, block)], s_loc.at[2]
        )

    each(0, n_x, lambda i: xe_copy(i).start())

    pl.semaphore_wait(bar, (n_chip - 1) + 2 * (n_seg - 1) + 1 + 2 * (n_seg + n_x) - jnp.where(not_diag, 0, 4))

    def e_up_from(j):
        return (j < n_seg - 1) & ((c == 0) & (j == 0) | (c == 1) & (j >= 1) | (c == up_core))

    def e_dn_from(j):
        return j >= 1 + c

    def e_up_copy(slot, peer):
        return remote(up_hbm.at[piece_of(peer), :], e_up.at[slot], eu_s.at[peer], eu_r.at[slot], peer, dp)

    def e_dn_copy(slot, peer):
        return remote(down_hbm.at[:, piece_of(peer)], e_dn.at[slot], ed_s.at[peer], ed_r.at[slot], peer, dp)

    for i in range(1, n_seg):
        peer = (r + i) % n_seg

        @pl.when(e_up_from(r))
        def _():
            e_up_copy(r, peer).start()

        @pl.when(e_dn_from(r))
        def _():
            e_dn_copy(r, peer).start()

    def xp_copy(i, slot_core, col_core):
        return remote(
            x_hbm.at[:, own_cols(i, col_core)],
            xs.at[slot_core, :, pl.ds(i * block, block)],
            xp_s,
            xp_r,
            r,
            partner,
        )

    each(0, n_x, lambda i: xp_copy(i, c, oc).start())

    pltpu.make_async_copy(down_hbm, dv, s_d).wait()
    acc[...] = jnp.zeros_like(acc)
    x_copy.wait()

    def a_step(i):
        sl = pl.ds(pl.multiple_of(i * kc, 128), kc)
        acc[...] += dot(xv[:, sl], dv[:, sl], NT)

    each(0, chunks, a_step)
    a_all[r] = acc[...]

    def seg_copy(buf, send, recv, slot, peer):
        return remote(buf.at[slot], buf.at[slot], send, recv, peer, dp)


    behind, ahead = (r + n_seg - 1) % n_seg, (r + 1) % n_seg
    first_rows, last_rows = pl.ds(0, tokens // 2), pl.ds(tokens // 2, tokens // 2)

    def near(buf, send, recv):
        remote(buf.at[r], buf.at[r], send.at[0], recv.at[0], ahead, dp).start()
        remote(buf.at[r], buf.at[r], send.at[0], recv.at[0], behind, dp).start()

    def pass_on(buf, send, recv):
        all_in(buf.at[pl.ds(0, 2)], recv.at[0])
        up_ref = buf.at[behind, first_rows]
        down_ref = buf.at[ahead, last_rows]
        remote(up_ref, up_ref, send.at[1], recv.at[1], ahead, dp).start()
        remote(down_ref, down_ref, send.at[1], recv.at[1], behind, dp).start()

    near(a_all, a_s, a_r)

    three = pl.ds(0, n_seg - 1)
    others = pl.ds(0, n_chip - 1)

    for j in range(n_seg):
        @pl.when((j != r) & e_up_from(j))
        def _():
            e_up_copy(j, (r + 1) % n_seg).wait_recv()

        @pl.when((j != r) & e_dn_from(j))
        def _():
            e_dn_copy(j, (r + 1) % n_seg).wait_recv()

    own_dn().wait()
    own_up().wait()
    e_rows = e_part.shape[1]
    e_mats = []
    for m, (da, ua) in enumerate(((2, 1), (3, 1), (3, 2))):
        e_mats.append(dot(e_dn[(1 - c) * (m + 1) + c * da], e_up[c * ua], NN))
    e_part[...] = jnp.concatenate(e_mats, axis=0).reshape(n_chip, e_rows, rank)

    def er_copy(slot, n):
        return remote(e_part.at[n], e_rs.at[slot], er_s, er_r, r, chip(n))

    each(1, n_chip, lambda i: er_copy(k, (k + i) % n_chip).start())

    def up_slot(n):
        return up_cat.at[pl.ds(pl.multiple_of((n // (2 * per)) * block + (n % per) * piece, 128), piece)]

    def ue_copy(slot, n):
        return remote(e_cat, up_slot(slot), ue_s, ue_r, r, chip(n))

    @pl.when(c == up_core)
    def _():
        for j in range(n_seg - 1):
            e_cat[:, j * rank:(j + 1) * rank] = e_up[j]
        each(1, n_chip, lambda i: ue_copy(k, (k + i) % n_chip).start())
        up_slot(k)[...] = e_cat[...]

    pltpu.make_async_copy(up_hbm, uv, s_u).wait()
    acc[...] = jnp.zeros_like(acc)
    c_copy.wait()

    def b_step(i):
        sl = pl.ds(pl.multiple_of(i * kc, 128), kc)
        acc[...] += dot(cv[:, sl], uv[sl, :], NN)

    each(0, chunks, b_step)
    b_all[r] = acc[...]

    e_rs[k] = e_part[k]
    all_in(e_rs.at[others], er_r)
    total = e_rs[0]
    for n in range(1, n_chip):
        total = total + e_rs[n]
    e_seg[r] = total
    for i in range(1, n_seg):
        seg_copy(e_seg, ey_s, ey_r, r, (r + i) % n_seg).start()
    near(b_all, b_s, b_r)
    lane = lax.broadcasted_iota(jnp.int32, (1, 128), 1)

    def count(i, total):
        return total + jnp.where(lane == ids[i], 1.0, 0.0)

    small(ids_hbm, ids, 0).wait()
    small(prior_hbm, prior, 1).wait()
    counts = lax.fori_loop(0, ids.shape[0], count, jnp.zeros((1, 128), F32))
    scale = 1.0 / (counts * TOK_MICRO)
    micros = 2 * tokens // TOK_MICRO

    def fill(m):
        name = ids[k * micros + m]
        row = jnp.where(lane == name, scale, 0.0)
        hot[pl.ds(pl.multiple_of(m * TOK_MICRO, 8), TOK_MICRO), :] = jnp.broadcast_to(row, (TOK_MICRO, 128))

    each(0, micros, fill)

    def set_rows(weights):
        for h in range(2):
            row_w[h] = lax.dot_general(
                weights,
                hot[h * tokens:(h + 1) * tokens, :],
                NT,
                precision=lax.Precision.HIGHEST,
                preferred_element_type=F32,
            )

    lane8 = lax.broadcasted_iota(jnp.int32, (8, 128), 1)
    gen_scale = jnp.sum(jnp.where(lane == DOMAINS - 1, scale, 0.0), axis=1, keepdims=True)
    set_rows(jnp.where(lane8 == DOMAINS - 1, 1.0, 0.0))
    for h in range(2):
        row_w[h] = jnp.where(row_w[h] > 0.0, 1.0, 0.0)

    all_in(e_seg.at[three], ey_r)
    e_all[c, k] = e_seg[0] + e_seg[1] + e_seg[2] + e_seg[3]

    def ea_copy(slot, n):
        return remote(e_all.at[c, slot], e_all.at[c, slot], ea_s, ea_r, r, chip(n))

    each(1, n_chip, lambda i: ea_copy(k, (k + i) % n_chip).start())

    pass_on(a_all, a_s, a_r)

    all_in(e_all.at[c, others], ea_r)

    def ep_copy(core):
        return remote(e_all.at[core], e_all.at[core], ep_s, ep_r, r, partner)

    ep_copy(c).start()
    pass_on(b_all, b_s, b_r)
    ep_copy(oc).wait_recv()

    all_in(a_all.at[0], a_r.at[1])

    def two_terms(m):
        high_part = m.astype(BF16)
        return high_part, (m - high_part.astype(F32)).astype(BF16)

    lower = {}
    for core, pairs in ((0, ((1, 0), (2, 0), (3, 0))), (1, ((2, 1), (3, 1), (3, 2)))):
        mats = e_all[core].reshape(3 * rank, rank)
        for m, pair in enumerate(pairs):
            lower[pair] = two_terms(mats[m * rank:(m + 1) * rank])

    def act_copy(j, core):
        ref = act_cat.at[core, :, pl.ds(j * rank, rank)]
        return remote(ref, ref, ac_s, ac_r, r, partner)

    def in_copy(core):
        return remote(inner_cat.at[core], inner_cat.at[core], in_s, in_r, r, partner)

    def it_copy(j, core):
        ref = inner_t.at[core, pl.ds(j * rank, rank)]
        return remote(ref, ref, it_s, it_r, r, partner)

    slopes = []
    acts = []
    for s in range(n_seg):
        pre = a_all[s]
        for j in range(s):
            pre = pre + dot(acts[j], lower[(s, j)][0], NT) + dot(acts[j], lower[(s, j)][1], NT)
        sig = 1.0 / (1.0 + jnp.exp(-pre))
        slopes.append(sig * (1.0 + pre * (1.0 - sig)))
        if s < n_seg - 1:
            act = (pre * sig).astype(BF16)
            acts.append(act)
            act_cat[c, :, s * rank:(s + 1) * rank] = act
            act_copy(s, c).start()

    all_in(b_all.at[0], b_r.at[1])

    inners = [None] * n_seg
    for s in reversed(range(n_seg)):
        pulled = b_all[s]
        for j in range(s + 1, n_seg):
            pulled = pulled + dot(inners[j], lower[(j, s)][0], NN) + dot(inners[j], lower[(j, s)][1], NN)
        wide = pulled * slopes[s]
        inner = wide.astype(BF16)
        inners[s] = inner
        inner_t[c, s * rank:(s + 1) * rank, :] = wide.T.astype(BF16)
        it_copy(s, c).start()
        inner_cat[c, :, s * rank:(s + 1) * rank] = inner

    in_copy(c).start()

    all_in(xs.at[c], s_loc.at[2])
    all_in(xs.at[oc], xp_r)

    @pl.when(c == up_core)
    def _():
        all_in(up_cat.at[pl.ds(0, n_x * block - piece)], ue_r)

    @pl.when(c != up_core)
    def _():
        all_in(up_cat, ue_r)

    all_in(act_cat.at[oc], ac_r)
    all_in(inner_t.at[oc], it_r)
    stack = n_seg * rank
    lower_mask = (
        lax.broadcasted_iota(jnp.int32, (stack, stack - rank), 0) // rank
        > lax.broadcasted_iota(jnp.int32, (stack, stack - rank), 1) // rank
    )

    def set_weighted():
        for h in range(2):
            weight = row_w[h, 0:1, :]
            for s in range(n_seg):
                rows = slice(s * rank, (s + 1) * rank)
                lhs_t[h, rows, :] = (inner_t[h, rows, :].astype(F32) * weight).astype(BF16)
        both = dot(lhs_t[0], act_cat[0], NN) + dot(lhs_t[1], act_cat[1], NN)
        cross[...] = jnp.where(lower_mask, both, 0.0).astype(BF16)

    def weighted_grad(i):
        sl = pl.ds(pl.multiple_of(i * block, 128), block)
        total = dot(lhs_t[0], xs[0, :, sl], NN) + dot(lhs_t[1], xs[1, :, sl], NN)
        return total + dot(cross[...], up_cat[pl.ds(pl.multiple_of(i * block, 128), block), :], NT)

    def first_a(send, recv, ss, rs, slot, i):
        return remote(send.at[i, :, low], recv.at[slot], ss.at[0], rs.at[0], r, chip(z * n_x + i))

    def first_b(send, recv, ss, rs, slot, j):
        return remote(send.at[:, j, high], recv.at[slot], ss.at[1], rs.at[1], r, chip(j * n_x + xx))

    def spread(send, recv_a, recv_b, ss, rs, factor):
        set_weighted()

        def column_block(t):
            i = (xx + 1 + t) % n_x
            send[i] = (weighted_grad(i) * factor).reshape(n_seg, rank, block).astype(BF16)

            @pl.when(i != xx)
            def _():
                first_a(send, recv_a, ss, rs, xx, i).start()

        each(0, n_x, column_block)
        for t in range(1, n_seg):
            first_b(send, recv_b, ss, rs, z, z_peer(t)).start()

    def pick(count):
        return pl.ds(0, count - 1)

    def join(ref, sem, axis_len):
        if axis_len > 1:
            all_in(ref, sem)

    def total_of(ref, count):
        total = ref[0].astype(F32)
        for i in range(1, count):
            total = total + ref[i].astype(F32)
        return total

    def sum_a(send, recv_a, rs):
        recv_a[xx] = send[xx, :, :half]
        join(recv_a.at[pick(n_x)], rs.at[0], n_x)
        return total_of(recv_a, n_x).astype(BF16)

    def sum_b(send, recv_b, rs):
        recv_b[z] = send[:, z, half:]
        join(recv_b.at[pick(n_seg)], rs.at[1], n_seg)
        return total_of(recv_b, n_seg).astype(BF16)

    spread(g_send, g_ra, g_rb, g_s, g_r, gen_scale)
    g_sa[...] = sum_a(g_send, g_ra, g_r)

    def second_a(slot, j):
        return remote(g_sa.at[j], g_ra2.at[slot], g_s.at[2], g_r.at[2], r, chip(j * n_x + xx))

    def second_b(slot, i):
        return remote(g_sb.at[i], g_rb2.at[slot], g_s.at[3], g_r.at[3], r, chip(z * n_x + i))

    for t in range(1, n_seg):
        second_a(z, z_peer(t)).start()
    g_sb[...] = sum_b(g_send, g_rb, g_r)
    for t in range(1, n_x):
        second_b(xx, x_peer(t)).start()
    g_ra2[z] = g_sa[z]
    join(g_ra2.at[pick(n_seg)], g_r.at[2], n_seg)
    total = total_of(g_ra2, n_seg)
    g_all[xx, z, :half] = total.astype(BF16)

    def gather(stage, slot, i, j):
        if stage == 0:
            ref, to = g_all.at[slot, z, low], z * n_x + i
        elif stage == 1:
            ref, to = g_all.at[xx, slot, high], j * n_x + xx
        elif stage == 2:
            ref, to = g_all.at[:, slot, low], j * n_x + xx
        else:
            ref, to = g_all.at[slot, :, high], z * n_x + i
        return remote(ref, ref, h_s.at[stage], h_r.at[stage], r, chip(to))

    for t in range(1, n_x):
        gather(0, xx, x_peer(t), z).start()
    g_rb2[xx] = g_sb[xx]
    join(g_rb2.at[pick(n_x)], g_r.at[3], n_x)
    total = total_of(g_rb2, n_x)
    g_all[xx, z, half:] = total.astype(BF16)
    for t in range(1, n_seg):
        gather(1, z, xx, z_peer(t)).start()

    join(g_all.at[pick(n_x), z, low], h_r.at[0], n_x)
    for t in range(1, n_seg):
        gather(2, z, xx, z_peer(t)).start()
    join(g_all.at[xx, pick(n_seg), high], h_r.at[1], n_seg)
    for t in range(1, n_x):
        gather(3, xx, x_peer(t), z).start()
    join(g_all.at[:, pick(n_seg), low], h_r.at[2], n_seg)

    y0 = jnp.zeros((tokens, stack), F32)
    y1 = jnp.zeros((tokens, stack), F32)
    gu = jnp.zeros((stack, stack - rank), F32)
    for t in range(n_x):
        i = x_peer(t)
        if t == 1:
            join(g_all.at[pick(n_x), :, high], h_r.at[3], n_x)
        grad = g_all[i].reshape(stack, block)
        sl = pl.ds(pl.multiple_of(i * block, 128), block)
        y0 = y0 + dot(xs[0, :, sl], grad, NT)
        y1 = y1 + dot(xs[1, :, sl], grad, NT)
        gu = gu + dot(grad, up_cat[sl, :], NN)
    gu = jnp.where(lower_mask, gu, 0.0).astype(BF16)
    in_copy(oc).wait_recv()
    mine = jnp.zeros((1, 128), F32)
    for h, y in ((0, y0), (1, y1)):
        y = (y + dot(act_cat[h], gu, NT)) * inner_cat[h].astype(F32)
        row = jnp.sum(y, axis=1, keepdims=True)
        mine = mine + jnp.sum(hot[h * tokens:(h + 1) * tokens, :] * row, axis=0, keepdims=True)
    sc0[...] = jnp.broadcast_to(mine, (8, 128))

    def p_copy(slot, n):
        return remote(sc0, sc1.at[slot], p_s, p_r, r, chip(n))

    for i in range(1, n_chip):
        p_copy(k, (k + i) % n_chip).start()

    sc1[k] = sc0[...]
    all_in(sc1.at[others], p_r)
    plane = total_of(sc1, n_chip)
    sc1s[...] = plane

    def q_copy(slot, n):
        return remote(sc1s, sc2.at[slot], q_s, q_r, n // 2, k * 2 + n % 2)

    here = r * 2 + c
    for i in range(1, 2 * n_seg):
        q_copy(here, (here + i) % (2 * n_seg)).start()

    sc2[here] = plane
    all_in(sc2.at[pl.ds(0, 2 * n_seg - 1)], q_r)
    scores = total_of(sc2, 2 * n_seg)

    entries = n_seg * rank * width
    mean_gen = jnp.sum(jnp.where(lane8 == DOMAINS - 1, scores, 0.0), axis=1, keepdims=True) / entries
    zed = scores / (math.sqrt(entries) * (mean_gen + 1e-06))
    prior_row = jnp.zeros((8, 128), F32)
    for i in range(DOMAINS - 1):
        prior_row = jnp.where(lane8 == i, prior[i], prior_row)
    train = lane8 < DOMAINS - 1
    raised = jnp.where(train, prior_row * jnp.exp(4.0 * jnp.tanh(zed / 4.0)), 0.0)
    weights = SMOOTHING / (DOMAINS - 1) + (1.0 - SMOOTHING) * raised / jnp.sum(raised, axis=1, keepdims=True)
    weights = jnp.where(train, weights, 0.0)
    set_rows(weights)

    spread(f_send, f_ra, f_rb, f_s, f_r, 1.0)
    for i in range(DOMAINS - 1):
        wout[i] = jnp.sum(jnp.where(lane == i, weights[0:1], 0.0))
    small(wout, wout_hbm, 0).start()

    def last_a(slot, s):
        return remote(f_sa.at[s], f_ra2.at[slot], f_s.at[2], f_r.at[2], s, chip(r * n_x + xx))

    def last_b(slot, i):
        return remote(f_sb.at[i], f_rb2.at[slot], f_s.at[3], f_r.at[3], z, chip(r * n_x + i))

    f_sa[...] = sum_a(f_send, f_ra, f_r)
    for t in range(1, n_seg):
        last_a(z, z_peer(t)).start()

    @pl.when(not_diag)
    def _():
        last_a(z, z).start()

    @pl.when(z == r)
    def _():
        f_ra2[z] = f_sa[z]

    f_sb[...] = sum_b(f_send, f_rb, f_r)
    for t in range(1, n_x):
        last_b(xx, x_peer(t)).start()

    @pl.when(not_diag)
    def _():
        last_b(xx, xx).start()

    @pl.when(z == r)
    def _():
        f_rb2[xx] = f_sb[xx]

    def join_last(ref, sem, count):
        @pl.when(not_diag)
        def _():
            all_in(ref, sem)

        @pl.when(z == r)
        def _():
            join(ref.at[pick(count)], sem, count)

    join_last(f_ra2, f_r.at[2], n_seg)
    rout[:half] = total_of(f_ra2, n_seg)
    small(rout.at[low], rout_hbm.at[low], 1).start()
    join_last(f_rb2, f_r.at[3], n_x)
    rout[half:] = total_of(f_rb2, n_x)
    small(rout.at[high], rout_hbm.at[high], 2).start()

    for i in range(1, n_seg):
        peer = (r + i) % n_seg

        @pl.when(e_up_from(r))
        def _():
            e_up_copy(r, peer).wait_send()

        @pl.when(e_dn_from(r))
        def _():
            e_dn_copy(r, peer).wait_send()


    for buf, sems in ((a_all, a_s), (b_all, b_s)):
        all_in(buf.at[pl.ds(0, 2)], sems.at[0])
        all_in(buf.at[0], sems.at[1])
    all_in(e_seg.at[three], ey_s)
    all_in(xs.at[c], xp_s)
    ep_copy(c).wait_send()
    all_in(act_cat.at[c], ac_s)
    all_in(inner_t.at[c], it_s)
    in_copy(c).wait_send()
    all_in(e_part.at[others], er_s)
    all_in(e_all.at[c, others], ea_s)
    all_in(sc1.at[others], p_s)
    all_in(sc2.at[pl.ds(0, 2 * n_seg - 1)], q_s)

    @pl.when(c == up_core)
    def _():
        all_in(uv.at[pl.ds(0, (n_chip - 1) * piece * (n_seg - 1))], ue_s)

    for send, sems in ((g_send, g_s), (f_send, f_s)):
        join(send.at[pick(n_x), :, low], sems.at[0], n_x)
        join(send.at[:, pick(n_seg), high], sems.at[1], n_seg)
    join(g_sa.at[pick(n_seg)], g_s.at[2], n_seg)
    join(g_sb.at[pick(n_x)], g_s.at[3], n_x)
    join(g_all.at[pick(n_x), z, low], h_s.at[0], n_x)
    join(g_all.at[xx, pick(n_seg), high], h_s.at[1], n_seg)
    join(g_all.at[:, pick(n_seg), low], h_s.at[2], n_seg)
    join(g_all.at[pick(n_x), :, high], h_s.at[3], n_x)
    join_last(f_sa, f_s.at[2], n_seg)
    join_last(f_sb, f_s.at[3], n_x)
    small(wout, wout_hbm, 0).wait()
    small(rout.at[low], rout_hbm.at[low], 1).wait()
    small(rout.at[high], rout_hbm.at[high], 2).wait()


def hand_over(weights, grad, wout, rout):
    for i in range(DOMAINS - 1):
        wout[i] = weights[i]
    rout[0] = grad[...]


def local(n_dp, inputs, cotangent, adapter_down, adapter_up, domain_ids, prior_weights):
    n_seg = 4
    n_chip = n_dp // 2
    n_x = n_chip // n_seg
    tokens, width = inputs.shape
    rank = adapter_down.shape[1]
    block = width // n_dp
    cols = n_x * block
    half = rank // 2
    e_rows = 3 * rank // n_chip
    down = adapter_down[0]
    up = adapter_up[0]
    piece = width // (n_seg * n_chip)
    dma = pltpu.SemaphoreType.DMA
    any_space = pl.BlockSpec(memory_space=pl.ANY)
    exchange = [
        pltpu.VMEM((n_x, n_seg, rank, block), BF16),
        pltpu.VMEM((n_x, n_seg, half, block), BF16),
        pltpu.VMEM((n_seg, n_x, half, block), BF16),
        pltpu.VMEM((n_seg, half, block), BF16),
        pltpu.VMEM((n_x, half, block), BF16),
        pltpu.VMEM((n_seg, half, block), BF16),
        pltpu.VMEM((n_x, half, block), BF16),
    ]
    scratch = [
        pltpu.SMEM(domain_ids.shape, jnp.int32),
        pltpu.SMEM(prior_weights.shape, F32),
        pltpu.SMEM((DOMAINS - 1,), F32),
        pltpu.VMEM((rank, block), F32),
        pltpu.VMEM((tokens, width), BF16),
        pltpu.VMEM((tokens, width), BF16),
        pltpu.VMEM((rank, width), BF16),
        pltpu.VMEM((width, rank), BF16),
        pltpu.VMEM((tokens, rank), F32),
        pltpu.VMEM((n_seg, piece, rank), BF16),
        pltpu.VMEM((n_seg, rank, piece), BF16),
        pltpu.VMEM((piece, 3 * rank), BF16),
        pltpu.VMEM((n_chip, e_rows, rank), F32),
        pltpu.VMEM((n_chip, e_rows, rank), F32),
        pltpu.VMEM((n_seg, e_rows, rank), F32),
        pltpu.VMEM((2, n_chip, e_rows, rank), F32),
        pltpu.VMEM((n_seg, tokens, rank), F32),
        pltpu.VMEM((n_seg, tokens, rank), F32),
        pltpu.VMEM((2, tokens, 3 * rank), BF16),
        pltpu.VMEM((2, tokens, 4 * rank), BF16),
        pltpu.VMEM((2, 4 * rank, tokens), BF16),
        pltpu.VMEM((n_x * block, 3 * rank), BF16),
        pltpu.VMEM((2, tokens, cols), BF16),
        pltpu.VMEM((2 * tokens, 128), F32),
        pltpu.VMEM((2, 8, tokens), F32),
        pltpu.VMEM((2, 4 * rank, tokens), BF16),
        pltpu.VMEM((4 * rank, 3 * rank), BF16),
        *exchange,
        pltpu.VMEM((n_x, n_seg, rank, block), BF16),
        pltpu.VMEM((8, 128), F32),
        pltpu.VMEM((n_chip, 8, 128), F32),
        pltpu.VMEM((8, 128), F32),
        pltpu.VMEM((2 * n_seg, 8, 128), F32),
        *exchange,
        dma, dma, dma, dma, dma((3,)), dma((3,)),
        dma((n_seg,)), dma((n_seg,)), dma((n_seg,)), dma((n_seg,)),
        dma, dma, dma, dma, dma, dma, dma, dma,
        dma((2,)), dma((2,)), dma((2,)), dma((2,)), dma, dma, dma, dma,
        dma, dma, dma, dma, dma, dma,
        dma((4,)), dma((4,)), dma((4,)), dma((4,)),
        dma, dma, dma, dma,
        dma((4,)), dma((4,)),
    ]
    weights, grad = pl.pallas_call(
        kernel,
        out_shape=(
            jax.ShapeDtypeStruct((DOMAINS - 1,), F32),
            jax.ShapeDtypeStruct((rank, block), F32),
        ),
        in_specs=[any_space] * 6,
        out_specs=(any_space, any_space),
        scratch_shapes=scratch,
        compiler_params=pltpu.CompilerParams(
            collective_id=0, has_side_effects=True, vmem_limit_bytes=56 * 1024 * 1024
        ),
    )(inputs, cotangent, down, up, domain_ids, prior_weights)
    return pl.pallas_call(
        hand_over,
        out_shape=(
            jax.ShapeDtypeStruct((DOMAINS - 1,), F32),
            jax.ShapeDtypeStruct((1, rank, block), F32),
        ),
        in_specs=[pl.BlockSpec(memory_space=pltpu.SMEM), pl.BlockSpec(memory_space=pltpu.VMEM)],
        out_specs=(pl.BlockSpec(memory_space=pltpu.SMEM), pl.BlockSpec(memory_space=pltpu.VMEM)),
    )(weights, grad)


def solution(mesh):
    return jax.shard_map(
        functools.partial(local, mesh.shape["dp"]),
        mesh=mesh,
        in_specs=(
            P("dp", None),
            P("dp", None),
            P("segment", None, None),
            P("segment", None, None),
            P(),
            P(),
        ),
        out_specs=(P(), P("segment", None, "dp")),
        check_vma=False,
    )
```
